128 devices in a mesh: member: 8 (over y_lo, x), grid: 16 (over y_hi, z, core).
Axes of the slice: x: 4, y: 4 (y_hi: 2, y_lo: 2; y = y_hi * 2 + y_lo), z: 4, core: 2. Of those that a mesh axis runs over, the one named last changes fastest.
Arguments:
- embedding_tensor: bfloat16 [16, 1024, 16384], P('member', None, 'grid'), may hold values from -6 to 6
- first_projection_matrix: bfloat16 [1024, 1024], replicated, may hold values from -0.1875 to 0.1875
- variable_projection_matrix: bfloat16 [1024, 100], replicated, may hold values from -0.1875 to 0.1875
- target: bfloat16 [100, 16384], P(None, 'grid'), may hold values from -5 to 5
- var_weight: float32 [100], replicated, may hold values from 0.3 to 3
- area_weight: float32 [16384], P('grid'), may hold values from 0.06 to 1.8, as said below
Outputs:
- embedding_derivative: bfloat16 [16, 1024, 16384], P('member', None, 'grid')
- grad_in: float32 [1024, 1024], replicated
- grad_out: float32 [1024, 100], replicated
- crps_penalty: float32 [], replicated
The draws below stay inside these ranges and needn't reach their ends.
Inputs may be any that keep to these rules, and one draw needn't show every extreme that they name: `area_weight`: area weights are positive.
All inputs are finite; a program needn't handle non-finite values.
Results may differ from the reference program's by a relative error of at most 0.003.
The reference program's roundings to bfloat16 on the way count: a program that leaves them out, or rounds other values in their place, can miss the bound.
Values sent between devices are 32-bit elements; how exact they have to be, the bound alone decides.
A program may use at most 128 MiB of HBM per device.

```python
import math
import jax
import jax.numpy as jnp
from jax import lax

H = 1024
V = 100
MEMBERS = 16
CELLS = 16384


def draw_area_weight(key, part):
    key = jax.random.fold_in(key, 11)
    position = jnp.arange(CELLS, dtype=jnp.float32)
    profile = 0.3 + 0.7 * jnp.sin(jnp.pi * (position + 0.5) / CELLS)
    rough = jax.random.uniform(key, (CELLS,), jnp.float32, 0.5, 1.5)
    return profile * rough


def levels(stream_key, dims, cuts, least, top_value):
    factor_of = 1.0
    for dim, blocks in cuts:
        draws = jax.random.uniform(jax.random.fold_in(jax.random.fold_in(stream_key, 6), dim), (blocks,), jnp.float32, least / len(cuts), top_value / len(cuts))
        factor_of = factor_of * jnp.repeat(jnp.exp(draws), dims[dim] // blocks).reshape((-1,) + (1,) * (len(dims) - 1 - dim))
    return factor_of


def bell_draw(rng, dims, deviation, reach, pieces=(), kind=jnp.bfloat16):
    result = jax.random.normal(rng, dims, jnp.float32) * deviation
    if len(pieces) > 0:
        result = levels(rng, dims, pieces, -0.22, 0.18) * result
    return jnp.clip(result, min=-reach, max=reach).astype(kind)


def setup_inputs(seed: int = 0) -> dict:
    seeds = jax.random.split(jax.random.key(seed), 7)
    return {
        "embedding_tensor": bell_draw(seeds[0], (MEMBERS, H, CELLS), 1.0, 6.0, ((0, 8), (2, 16))),
        "first_projection_matrix": bell_draw(seeds[1], (H, H), H ** -0.5, 0.1875),
        "variable_projection_matrix": bell_draw(seeds[2], (H, V), H ** -0.5, 0.1875),
        "target": bell_draw(seeds[3], (V, CELLS), 0.7, 5.0, ((1, 16),)),
        "var_weight": jnp.clip(jnp.exp(jax.random.uniform(seeds[4], (V,), jnp.float32, math.log(0.3), math.log(3.0))), 0.3, 3.0),
        "area_weight": draw_area_weight(jax.random.fold_in(seeds[6], 71), 0),
    }


SMOOTH_WIDTH = 0.1
ALPHA_FAIR = 0.95

def magnitude_derivative(values):
    return values * lax.rsqrt(values * values + SMOOTH_WIDTH * SMOOTH_WIDTH)

def softened_magnitude(values):
    return jnp.sqrt(values * values + SMOOTH_WIDTH * SMOOTH_WIDTH) - SMOOTH_WIDTH

def map_embedding_back(ensemble_entry_embedding, first_projection_matrix, variable_projection_matrix):
    intermediate_linear_sum = jnp.dot(first_projection_matrix.T, ensemble_entry_embedding, preferred_element_type=jnp.float32)
    intermediate_response = jax.nn.gelu(intermediate_linear_sum).astype(jnp.bfloat16)
    lone_estimate = jnp.dot(variable_projection_matrix.T, intermediate_response, preferred_element_type=jnp.float32)
    return (intermediate_linear_sum, intermediate_response, lone_estimate)

def reference(embedding_tensor, first_projection_matrix, variable_projection_matrix, target, var_weight, area_weight):
    members = embedding_tensor.shape[0]
    unbiased_blend_factor = (1.0 - (1.0 - ALPHA_FAIR) / members) / (members - 1)
    mean_area = jnp.sum(area_weight) / CELLS
    variable_normaliser = (area_weight / mean_area)[None, :] * var_weight[:, None]
    verifying_truth = target.astype(jnp.float32)
    ensemble_predictions_array = lax.map(lambda ensemble_entry_embedding: map_embedding_back(ensemble_entry_embedding, first_projection_matrix, variable_projection_matrix)[2], embedding_tensor)

    def ensemble_entry_update(carry, embedding_sources):
        grad_first, grad_second, spread_sum, truth_residual = carry
        ensemble_entry_embedding, ensemble_entry_prediction = embedding_sources
        intermediate_linear_sum, intermediate_response, unused_value = map_embedding_back(ensemble_entry_embedding, first_projection_matrix, variable_projection_matrix)
        pairwise_ensemble_gaps = ensemble_entry_prediction[None] - ensemble_predictions_array
        accumulated_derivative = lax.optimization_barrier(jnp.sum(magnitude_derivative(pairwise_ensemble_gaps), 0))
        spread_sum = spread_sum + lax.optimization_barrier(jnp.sum(softened_magnitude(pairwise_ensemble_gaps), 0))
        truth_residual = truth_residual + softened_magnitude(ensemble_entry_prediction - verifying_truth)
        estimate_derivative = (variable_normaliser * (magnitude_derivative(ensemble_entry_prediction - verifying_truth) - unbiased_blend_factor * accumulated_derivative)).astype(jnp.bfloat16)
        grad_second = grad_second + jnp.dot(intermediate_response, estimate_derivative.T, preferred_element_type=jnp.float32)
        grad_act = jnp.dot(variable_projection_matrix, estimate_derivative, preferred_element_type=jnp.float32)
        unused_out, backward = jax.vjp(jax.nn.gelu, intermediate_linear_sum)
        grad_pre = backward(grad_act)[0].astype(jnp.bfloat16)
        member_grad = jnp.dot(first_projection_matrix, grad_pre, preferred_element_type=jnp.float32).astype(jnp.bfloat16)
        grad_first = grad_first + jnp.dot(ensemble_entry_embedding, grad_pre.T, preferred_element_type=jnp.float32)
        return ((grad_first, grad_second, spread_sum, truth_residual), member_grad)
    start_position = (jnp.zeros((H, H), jnp.float32), jnp.zeros((H, V), jnp.float32), jnp.zeros((V, CELLS), jnp.float32), jnp.zeros((V, CELLS), jnp.float32))
    closing_results, embedding_derivative = lax.scan(ensemble_entry_update, start_position, (embedding_tensor, ensemble_predictions_array))
    grad_first, grad_second, spread_sum, truth_residual = closing_results
    crps_penalty = jnp.sum(variable_normaliser * (truth_residual / members - unbiased_blend_factor / (2 * members) * spread_sum)) / (CELLS * V)
    rescale = 1.0 / math.sqrt(members * CELLS)
    return (embedding_derivative, grad_first * rescale, grad_second * rescale, crps_penalty)
```

```python
import functools
import math

import jax
import jax.numpy as jnp
from jax import lax
from jax.experimental import pallas as pl
from jax.experimental.pallas import tpu as pltpu
from jax.sharding import PartitionSpec as P

SMOOTH_WIDTH = 0.1
ALPHA_FAIR = 0.95
MESH = pl.DeviceIdType.MESH
F32 = jnp.float32
BF16 = jnp.bfloat16
GELU_A = math.sqrt(2.0 / math.pi)
GELU_B = 0.044715

H = 1024
V = 100
VH = V // 2
VP = 128
CELLS = 1024
MEM = 2
TOTAL_MEM = 16
TOTAL_CELLS = 16384
NQ = 2
CQ = CELLS // NQ
HALF = H // 2
WIDE = H + VP
PW = WIDE // 3
LOSS_COL = 60
ORDERS = (("x", "y", "z"), ("y", "z", "x"), ("z", "x", "y"))
OFFSETS = (2, 1, 3)


def dot(a, b):
    return lax.dot_general(a, b, (((1,), (0,)), ((), ())), preferred_element_type=F32)


def dot_t(a, b):
    return lax.dot_general(a, b, (((1,), (1,)), ((), ())), preferred_element_type=F32)


def gelu_and_derivative(x):
    x2 = x * x
    t = jnp.tanh(x * (GELU_A + (GELU_A * GELU_B) * x2))
    h = 0.5 + 0.5 * t
    y = x * h
    return y, h + (y * (1.0 - t)) * (GELU_A + (3.0 * GELU_A * GELU_B) * x2)


def ds(start, size, multiple):
    return pl.ds(pl.multiple_of(start, multiple), size)


def kernel(
    emb, w1_hbm, w2, target, vw, aw,
    ed_out, wide_out,
    e, w1, w1t, w2p, w2t, act, dg, gv, gp, tgt, vcol, av,
    fs, fr, gs, gr, grad, core_in, s1, r1, s2, r2, s3, full, loss,
    in_sem, area_s, area_r, fs_s, fs_r, gs_s, gs_r, core_s, core_r,
    rs_s, rs_r, ag_s, ag_r, cg_s, cg_r, out_sem,
):
    me = lax.axis_index("member")
    g = lax.axis_index("grid")
    pos = {"x": me % 4, "y": (g // 8) * 2 + me // 4, "z": (g // 2) % 4, "c": g % 2}
    core = pos["c"]

    def device(p):
        return ((p["y"] % 2) * 4 + p["x"], ((p["y"] // 2) * 4 + p["z"]) * 2 + p["c"])

    def moved(**by):
        return {k: (v + by[k]) % (2 if k == "c" else 4) if k in by else v for k, v in pos.items()}

    def member_peer(o):
        return (me // 4 + o // 4) % 2 * 4 + (me % 4 + o % 4) % 4

    def member_from(o):
        return (me // 4 + o // 4) % 2 * 4 + (me % 4 + 4 - o % 4) % 4

    w1_copy = pltpu.make_async_copy(w1_hbm, w1, in_sem.at[4])
    w1_copy.start()

    def emb_copy(q, m):
        sl = pl.ds(q * CQ, CQ)
        return pltpu.make_async_copy(emb.at[m, :, sl], e.at[m, :, sl], in_sem.at[q * 2 + m])

    for q in range(NQ):
        for m in range(MEM):
            emb_copy(q, m).start()

    barrier = pltpu.get_barrier_semaphore()
    for o in range(1, 8):
        pl.semaphore_signal(barrier, inc=1, device_id=(member_peer(o), g), device_id_type=MESH)
    for o in range(1, 16):
        pl.semaphore_signal(barrier, inc=1, device_id=(me, (g + o) % 16), device_id_type=MESH)
    pl.semaphore_signal(
        barrier, inc=1, device_id=((me + 4) % 8, (g + 8) % 16), device_id_type=MESH
    )

    w2p[...] = jnp.zeros_like(w2p)
    w2p[:, 0:VH] = w2[:, 0:VH]
    w2p[:, 64 : 64 + VH] = w2[:, VH:V]
    w2t[...] = w2p[...].T
    t32 = target[...].astype(F32)
    tgt[0] = t32[0:VH]
    tgt[1] = t32[VH:V]
    columns = jnp.broadcast_to(vw[...], (VP, VP)).T
    vcol[0] = columns[0:VH]
    vcol[1] = columns[VH:V]
    av[g] = aw[...]
    loss[...] = jnp.zeros_like(loss)
    w1_copy.wait()
    w1t[...] = w1[...].T

    pl.semaphore_wait(barrier, 23)
    area_copies = []
    for o in range(1, 16):
        copy = pltpu.make_async_remote_copy(
            src_ref=av.at[g], dst_ref=av.at[g], send_sem=area_s.at[o], recv_sem=area_r.at[o],
            device_id=(me, (g + o) % 16), device_id_type=MESH,
        )
        copy.start()
        area_copies.append(copy)

    def exchange(q, o, src, dst, ss, rs):
        return pltpu.make_async_remote_copy(
            src_ref=src.at[q, member_peer(o)], dst_ref=dst.at[q, me],
            send_sem=ss.at[q, o], recv_sem=rs.at[q, o],
            device_id=(member_peer(o), g), device_id_type=MESH,
        )

    def exchange_in(q, o, src, dst, ss, rs):
        return pltpu.make_async_remote_copy(
            src_ref=src.at[q, member_peer(o)], dst_ref=dst.at[q, member_from(o)],
            send_sem=ss.at[q, o], recv_sem=rs.at[q, o],
            device_id=(member_peer(o), g), device_id_type=MESH,
        )

    PEERS = (6, 2, 5, 7, 4, 1, 3)

    def send_all(q, src, dst, ss, rs):
        for o in PEERS:
            exchange(q, o, src, dst, ss, rs).start()
        dst[q, me] = src[q, me]

    def receive_all(q, src, dst, ss, rs):
        for o in PEERS:
            exchange_in(q, o, src, dst, ss, rs).wait_recv()

    def forward(q):
        sl = pl.ds(q * CQ, CQ)

        @pl.loop(0, MEM)
        def _(m):
            emb_copy(q, m).wait()
            y, d = gelu_and_derivative(dot(w1t[...], e[m, :, sl]))
            act[m, :, sl] = y.astype(BF16)
            dg[m, :, sl] = d
            fc = dot(w2t[...], act[m, :, sl])
            for r in range(2):
                for l in range(4):
                    fs[q, r * 4 + l, m] = fc[64 * r : 64 * r + VH, 128 * l : 128 * l + 128]

        send_all(q, fs, fr, fs_s, fs_r)

    coef = (1.0 - (1.0 - ALPHA_FAIR) / TOTAL_MEM) / (TOTAL_MEM - 1)
    d2 = SMOOTH_WIDTH * SMOOTH_WIDTH

    def pairwise(q):
        mine_r, mine_l = me // 4, me % 4
        lanes = ds(q * CQ + mine_l * 128, 128, 128)
        mean = jnp.sum(jnp.sum(av[...], axis=0), keepdims=True) / TOTAL_CELLS
        area = aw[pl.ds(q * 4 + mine_l, 1), :] / mean

        def tile(rows, n):
            scale = area * vcol[mine_r, rows, :]
            t = tgt[mine_r, rows, lanes]
            f = [fr[q, k // 2, k % 2, rows, :] for k in range(TOTAL_MEM)]
            s = [None] * TOTAL_MEM
            spread = None
            for i in range(TOTAL_MEM):
                for k in range(i + 1, TOTAL_MEM):
                    d = f[i] - f[k]
                    w = d * d + d2
                    inv = lax.rsqrt(w)
                    slope = d * inv
                    s[i] = slope if s[i] is None else s[i] + slope
                    s[k] = -slope if s[k] is None else s[k] - slope
                    smooth = w * inv - SMOOTH_WIDTH
                    spread = smooth if spread is None else spread + smooth
            truth = None
            for i in range(TOTAL_MEM):
                d = f[i] - t
                w = d * d + d2
                inv = lax.rsqrt(w)
                gs[q, i // 2, i % 2, rows, :] = scale * (d * inv - coef * s[i])
                smooth = w * inv - SMOOTH_WIDTH
                truth = smooth if truth is None else truth + smooth
            loss[0:n, :] += scale * (truth / TOTAL_MEM - (coef / TOTAL_MEM) * spread)

        @pl.loop(0, VH // 8)
        def _(i):
            tile(ds(i * 8, 8, 8), 8)

        tile(pl.ds(VH // 8 * 8, VH % 8), VH % 8)
        send_all(q, gs, gr, gs_s, gs_r)

    def backward(q):
        sl = pl.ds(q * CQ, CQ)
        zeros = jnp.zeros((64 - VH, 128), F32)

        @pl.loop(0, MEM)
        def _(m):
            for r in range(2):
                for l in range(4):
                    block = jnp.concatenate([gr[q, r * 4 + l, m], zeros], axis=0)
                    gv[m, 64 * r : 64 * r + 64, q * CQ + 128 * l : q * CQ + 128 * l + 128] = (
                        block.astype(BF16)
                    )
            gp[m, :, sl] = (dot(w2p[...], gv[m, :, sl]) * dg[m, :, sl]).astype(BF16)

    def weight_gradients(q, half):
        sl = pl.ds(q * CQ, CQ)
        rows = ds(half * HALF, HALF, HALF)

        @pl.loop(0, 4)
        def _(j):
            cols = ds(j * 256, 256, 256)
            new = dot_t(e[0, rows, sl], gp[0, cols, sl]) + dot_t(e[1, rows, sl], gp[1, cols, sl])
            if q == 0:
                grad[rows, cols] = new
            else:
                grad[rows, cols] += new

        new = dot_t(act[0, rows, sl], gv[0, :, sl]) + dot_t(act[1, rows, sl], gv[1, :, sl])
        if q == 0:
            grad[rows, H:WIDE] = new
        else:
            grad[rows, H:WIDE] += new

    def embedding_derivative(m, q):
        sl = pl.ds(q * CQ, CQ)
        e[m, :, sl] = dot(w1[...], gp[m, :, sl]).astype(BF16)
        copy = pltpu.make_async_copy(e.at[m, :, sl], ed_out.at[m, :, sl], out_sem.at[q * 2 + m])
        copy.start()
        return copy

    def part_cols(p):
        return pl.ds(p * PW, PW)

    forward(0)
    forward(1)
    for copy in area_copies:
        copy.wait()
    receive_all(0, fs, fr, fs_s, fs_r)
    pairwise(0)
    receive_all(1, fs, fr, fs_s, fs_r)
    pairwise(1)
    receive_all(0, gs, gr, gs_s, gs_r)
    backward(0)
    weight_gradients(0, 0)
    weight_gradients(0, 1)
    receive_all(1, gs, gr, gs_s, gs_r)
    backward(1)
    weight_gradients(1, 1 - core)
    own_loss = jnp.sum(loss[...], keepdims=True)
    row = lax.broadcasted_iota(jnp.int32, (8, VP), 0)
    col = lax.broadcasted_iota(jnp.int32, (8, VP), 1)
    grad[0:8, H:WIDE] += jnp.where((row == 0) & (col == LOSS_COL), own_loss, 0.0)

    def core_copy(s, p, half):
        k = (pos[ORDERS[p][0]] + s) % 4
        return pltpu.make_async_remote_copy(
            src_ref=grad.at[ds(half * HALF + k * 128, 128, 128), part_cols(p)],
            dst_ref=core_in.at[ds(k * 128, 128, 128), part_cols(p)],
            send_sem=core_s.at[s, p], recv_sem=core_r.at[s, p],
            device_id=device(moved(c=1)), device_id_type=MESH,
        )

    steps = OFFSETS + (0,)
    for s in steps:
        for p in range(3):
            core_copy(s, p, 1 - core).start()
    weight_gradients(1, core)

    def block_rows(p, ks):
        start = core * HALF
        for k, size in zip(ks, (128, 32, 8)):
            start = start + k * size
        return start

    def rs1(s, p):
        axis = ORDERS[p][0]
        k = (pos[axis] + s) % 4
        return pltpu.make_async_remote_copy(
            src_ref=grad.at[ds(block_rows(p, [k]), 128, 128), part_cols(p)],
            dst_ref=s1.at[p, s - 1], send_sem=rs_s.at[0, p, s], recv_sem=rs_r.at[0, p, s],
            device_id=device(moved(**{axis: s})), device_id_type=MESH,
        )

    ed_copies = []
    tiles = [(0, 0), (1, 0), (0, 1), (1, 1)]
    for n, s in enumerate(steps):
        for p in range(3):
            core_copy(s, p, 1 - core).wait_recv()
            k = (pos[ORDERS[p][0]] + s) % 4
            rows = ds(block_rows(p, [k]), 128, 128)
            cols = part_cols(p)
            grad[rows, cols] += core_in[ds(k * 128, 128, 128), cols]
            if s:
                rs1(s, p).start()
        ed_copies.append(embedding_derivative(*tiles[n]))

    for p in range(3):
        for s in OFFSETS:
            rs1(s, p).wait_recv()
        k = pos[ORDERS[p][0]]
        rows = ds(block_rows(p, [k]), 128, 128)
        r1[p] = grad[rows, part_cols(p)] + s1[p, 0] + s1[p, 1] + s1[p, 2]

    def rs2(s, p):
        axis = ORDERS[p][1]
        k = (pos[axis] + s) % 4
        return pltpu.make_async_remote_copy(
            src_ref=r1.at[p, ds(k * 32, 32, 32)], dst_ref=s2.at[p, s - 1],
            send_sem=rs_s.at[1, p, s], recv_sem=rs_r.at[1, p, s],
            device_id=device(moved(**{axis: s})), device_id_type=MESH,
        )

    def rs3(s, p):
        axis = ORDERS[p][2]
        k = (pos[axis] + s) % 4
        return pltpu.make_async_remote_copy(
            src_ref=r2.at[p, ds(k * 8, 8, 8)], dst_ref=s3.at[p, s - 1],
            send_sem=rs_s.at[2, p, s], recv_sem=rs_r.at[2, p, s],
            device_id=device(moved(**{axis: s})), device_id_type=MESH,
        )

    for p in range(3):
        for s in OFFSETS:
            rs2(s, p).start()
    for p in range(3):
        for s in OFFSETS:
            rs2(s, p).wait_recv()
        k = pos[ORDERS[p][1]]
        r2[p] = r1[p, ds(k * 32, 32, 32)] + s2[p, 0] + s2[p, 1] + s2[p, 2]
        for s in OFFSETS:
            rs3(s, p).start()

    def gather_copy(level, p, s, arriving):
        axis = ORDERS[p][level]
        ks = [pos[a] for a in ORDERS[p][: level + 1]]
        if arriving:
            ks[level] = (ks[level] + 4 - s) % 4
        size = (128, 32, 8)[level]
        at = full.at[ds(block_rows(p, ks), size, size), part_cols(p)]
        return pltpu.make_async_remote_copy(
            src_ref=at, dst_ref=at, send_sem=ag_s.at[level, p, s], recv_sem=ag_r.at[level, p, s],
            device_id=device(moved(**{axis: s})), device_id_type=MESH,
        )

    rescale = 1.0 / math.sqrt(TOTAL_MEM * TOTAL_CELLS)
    for p in range(3):
        for s in OFFSETS:
            rs3(s, p).wait_recv()
        ks = [pos[a] for a in ORDERS[p]]
        total = r2[p, ds(ks[2] * 8, 8, 8)] + s3[p, 0] + s3[p, 1] + s3[p, 2]
        full[ds(block_rows(p, ks), 8, 8), part_cols(p)] = total * rescale
        for s in OFFSETS:
            gather_copy(2, p, s, False).start()

    for level in (2, 1):
        for p in range(3):
            for s in OFFSETS:
                gather_copy(level, p, s, True).wait_recv()
            for s in OFFSETS:
                gather_copy(level - 1, p, s, False).start()

    def block(p, s, c):
        k = (pos[ORDERS[p][0]] + 4 - s) % 4
        return (ds(c * HALF + k * 128, 128, 128), part_cols(p))

    def core_gather(p, s, c):
        at = full.at[block(p, s, c)]
        return pltpu.make_async_remote_copy(
            src_ref=at, dst_ref=at, send_sem=cg_s.at[p, s], recv_sem=cg_r.at[p, s],
            device_id=device(moved(c=1)), device_id_type=MESH,
        )

    out_copies = []

    def store(p, s, c, n):
        where = block(p, s, c)
        copy = pltpu.make_async_copy(full.at[where], wide_out.at[where], out_sem.at[4 + n])
        copy.start()
        out_copies.append(copy)

    for p in range(3):
        core_gather(p, 0, core).start()
        store(p, 0, core, p)
    for s in (1, 3, 2):
        for p in range(3):
            gather_copy(0, p, s, True).wait_recv()
            core_gather(p, s, core).start()
            store(p, s, core, s * 3 + p)
    for s in (0, 1, 3, 2):
        for p in range(3):
            core_gather(p, s, 1 - core).wait_recv()
            store(p, s, 1 - core, 12 + s * 3 + p)

    for q in range(NQ):
        for o in PEERS:
            exchange(q, o, fs, fr, fs_s, fs_r).wait_send()
            exchange(q, o, gs, gr, gs_s, gs_r).wait_send()
    for p in range(3):
        for s in steps:
            core_copy(s, p, 1 - core).wait_send()
            core_gather(p, s, core).wait_send()
        for s in OFFSETS:
            rs1(s, p).wait_send()
            rs2(s, p).wait_send()
            rs3(s, p).wait_send()
            for level in range(3):
                gather_copy(level, p, s, False).wait_send()
    for copy in ed_copies + out_copies:
        copy.wait()


def per_device(
    embedding_tensor,
    first_projection_matrix,
    variable_projection_matrix,
    target,
    var_weight,
    area_weight,
):
    vmem = pl.BlockSpec(memory_space=pltpu.VMEM)
    hbm = pl.BlockSpec(memory_space=pl.ANY)
    dma = pltpu.SemaphoreType.DMA
    big = (MEM, H, CELLS)
    swap = (NQ, 8, MEM, VH, 128)
    ed, wide = pl.pallas_call(
        kernel,
        name="decoder_crps",
        out_shape=(
            jax.ShapeDtypeStruct(big, BF16),
            jax.ShapeDtypeStruct((H, WIDE), F32),
        ),
        in_specs=[hbm, hbm, vmem, vmem, vmem, vmem],
        out_specs=(hbm, hbm),
        scratch_shapes=[
            pltpu.VMEM(big, BF16),
            pltpu.VMEM((H, H), BF16),
            pltpu.VMEM((H, H), BF16),
            pltpu.VMEM((H, VP), BF16),
            pltpu.VMEM((VP, H), BF16),
            pltpu.VMEM(big, BF16),
            pltpu.VMEM(big, F32),
            pltpu.VMEM((MEM, VP, CELLS), BF16),
            pltpu.VMEM(big, BF16),
            pltpu.VMEM((2, VH, CELLS), F32),
            pltpu.VMEM((2, VH, 128), F32),
            pltpu.VMEM((16, 8, 128), F32),
            pltpu.VMEM(swap, F32),
            pltpu.VMEM(swap, F32),
            pltpu.VMEM(swap, F32),
            pltpu.VMEM(swap, F32),
            pltpu.VMEM((H, WIDE), F32),
            pltpu.VMEM((HALF, WIDE), F32),
            pltpu.VMEM((3, 3, 128, PW), F32),
            pltpu.VMEM((3, 128, PW), F32),
            pltpu.VMEM((3, 3, 32, PW), F32),
            pltpu.VMEM((3, 32, PW), F32),
            pltpu.VMEM((3, 3, 8, PW), F32),
            pltpu.VMEM((H, WIDE), F32),
            pltpu.VMEM((8, 128), F32),
            dma((5,)),
            dma((16,)), dma((16,)),
            dma((NQ, 8)), dma((NQ, 8)),
            dma((NQ, 8)), dma((NQ, 8)),
            dma((4, 3)), dma((4, 3)),
            dma((3, 3, 4)), dma((3, 3, 4)),
            dma((3, 3, 4)), dma((3, 3, 4)),
            dma((3, 4)), dma((3, 4)),
            dma((28,)),
        ],
        compiler_params=pltpu.CompilerParams(
            collective_id=0, has_side_effects=True, vmem_limit_bytes=60 * 2**20
        ),
        cost_estimate=pl.CostEstimate(
            flops=15_000_000_000, bytes_accessed=20_000_000, transcendentals=4_000_000
        ),
    )(
        embedding_tensor,
        first_projection_matrix,
        variable_projection_matrix,
        target,
        jnp.pad(var_weight, (0, VP - V)).reshape(1, VP),
        area_weight.reshape(8, 128),
    )
    grad_out = jnp.concatenate([wide[:, H : H + VH], wide[:, H + 64 : H + 64 + VH]], axis=1)
    rescale = 1.0 / math.sqrt(TOTAL_MEM * TOTAL_CELLS)
    crps = wide[0, H + LOSS_COL] / (rescale * TOTAL_CELLS * V)
    return ed, wide[:, :H], grad_out, crps


def solution(mesh):
    in_specs = (P("member", None, "grid"), P(), P(), P(None, "grid"), P(), P("grid"))
    out_specs = (P("member", None, "grid"), P(), P(), P())
    return jax.shard_map(
        per_device, mesh=mesh, in_specs=in_specs, out_specs=out_specs, check_vma=False
    )
```

```python
import functools
import math

import jax
import jax.numpy as jnp
from jax import lax
from jax.experimental import pallas as pl
from jax.experimental.pallas import tpu as pltpu
from jax.sharding import PartitionSpec as P

SMOOTH_WIDTH = 0.1
ALPHA_FAIR = 0.95
MESH = pl.DeviceIdType.MESH
F32 = jnp.float32
BF16 = jnp.bfloat16
GELU_A = math.sqrt(2.0 / math.pi)
GELU_B = 0.044715

H = 1024
V = 100
VH = V // 2
VP = 128
CELLS = 1024
MEM = 2
TOTAL_MEM = 16
TOTAL_CELLS = 16384
NQ = 2
CQ = CELLS // NQ
HALF = H // 2
WIDE = H + VP
PW = WIDE // 3
LOSS_COL = 60
ORDERS = (("x", "y", "z"), ("y", "z", "x"), ("z", "x", "y"))
OFFSETS = (2, 1, 3)


def dot(a, b):
    return lax.dot_general(a, b, (((1,), (0,)), ((), ())), preferred_element_type=F32)


def dot_t(a, b):
    return lax.dot_general(a, b, (((1,), (1,)), ((), ())), preferred_element_type=F32)


def gelu_and_derivative(x):
    x2 = x * x
    t = jnp.tanh(x * (GELU_A + (GELU_A * GELU_B) * x2))
    h = 0.5 + 0.5 * t
    y = x * h
    return y, h + (y * (1.0 - t)) * (GELU_A + (3.0 * GELU_A * GELU_B) * x2)


def ds(start, size, multiple):
    return pl.ds(pl.multiple_of(start, multiple), size)


def kernel(
    emb, w1_hbm, w2_t, target, vw, aw,
    ed, full,
    e, w1, w1t, w2p, w2t, act, dg, gv, gp, tgt, vcol, av,
    fs, fr, gs, gr, grad, core_in, s1, r1, s2, r2, s3, loss,
    in_sem, area_s, area_r, fs_s, fs_r, gs_s, gs_r, core_s, core_r,
    rs_s, rs_r, ag_s, ag_r, cg_s, cg_r,
):
    me = lax.axis_index("member")
    g = lax.axis_index("grid")
    pos = {"x": me % 4, "y": (g // 8) * 2 + me // 4, "z": (g // 2) % 4, "c": g % 2}
    core = pos["c"]
    sent = {}

    def start(key, copy):
        copy.start()
        sent[key] = copy

    def arrived(key, copy):
        copy.wait_recv()

    def device(p):
        return ((p["y"] % 2) * 4 + p["x"], ((p["y"] // 2) * 4 + p["z"]) * 2 + p["c"])

    def moved(**by):
        return {k: (v + by[k]) % (2 if k == "c" else 4) if k in by else v for k, v in pos.items()}

    def remote(src, dst, send_sem, recv_sem, to):
        return pltpu.make_async_remote_copy(
            src_ref=src, dst_ref=dst, send_sem=send_sem, recv_sem=recv_sem,
            device_id=to, device_id_type=MESH,
        )

    def member_peer(o):
        return (me // 4 + o // 4) % 2 * 4 + (me % 4 + o % 4) % 4

    def member_from(o):
        return (me // 4 + o // 4) % 2 * 4 + (me % 4 + 4 - o % 4) % 4

    def emb_copy(q, m):
        sl = pl.ds(q * CQ, CQ)
        return pltpu.make_async_copy(emb.at[m, :, sl], e.at[m, :, sl], in_sem.at[q * 2 + m])

    def area_copy(o):
        return remote(av.at[g], av.at[g], area_s.at[o], area_r.at[o], (me, (g + o) % 16))

    def area_arrival(o):
        at = av.at[(g + 16 - o) % 16]
        return remote(at, at, area_s.at[o], area_r.at[o], (me, (g + o) % 16))

    def begin():
        w1_copy = pltpu.make_async_copy(w1_hbm, w1, in_sem.at[4])
        w1_copy.start()
        for q in range(NQ):
            for m in range(MEM):
                emb_copy(q, m).start()

        barrier = pltpu.get_barrier_semaphore()
        peers = [(member_peer(o), g) for o in range(1, 8)]
        peers += [(me, (g + o) % 16) for o in range(1, 16)]
        peers += [((me + 4) % 8, (g + 8) % 16)]
        for peer in peers:
            pl.semaphore_signal(barrier, inc=1, device_id=peer, device_id_type=MESH)

        w2t[...] = jnp.zeros_like(w2t)
        wide = w2_t[...].astype(F32)
        gap = jnp.zeros((64 - VH, H), F32)
        w2t[0:64] = jnp.concatenate([wide[0:VH], gap], axis=0).astype(BF16)
        w2t[64:VP] = jnp.concatenate([wide[VH:V], gap], axis=0).astype(BF16)
        w2p[...] = w2t[...].T
        t32 = target[...].astype(F32)
        tgt[0] = t32[0:VH]
        tgt[1] = t32[VH:V]
        columns = jnp.broadcast_to(vw[...], (VP, V)).T
        vcol[0] = columns[0:VH]
        vcol[1] = columns[VH:V]
        av[g] = aw[...]
        loss[...] = jnp.zeros_like(loss)
        w1_copy.wait()
        w1t[...] = w1[...].T

        pl.semaphore_wait(barrier, 23)
        for o in range(1, 16):
            start(("area", o), area_copy(o))

    def exchange(q, o, src, dst, ss, rs, arriving):
        slot = member_from(o) if arriving else me
        return remote(
            src.at[q, member_peer(o)], dst.at[q, slot], ss.at[q, o], rs.at[q, o],
            (member_peer(o), g),
        )

    PEERS = (6, 2, 5, 7, 4, 1, 3)
    FORECAST = (fs, fr, fs_s, fs_r)
    BACK = (gs, gr, gs_s, gs_r)

    def send_all(name, q, way):
        for o in PEERS:
            start((name, q, o), exchange(q, o, *way, False))
        src, dst = way[:2]
        dst[q, me] = src[q, me]

    def receive_all(name, q, way):
        for o in PEERS:
            arrived((name, q, o), exchange(q, o, *way, True))

    def forward(q):
        sl = pl.ds(q * CQ, CQ)

        @pl.loop(0, MEM)
        def _(m):
            emb_copy(q, m).wait()
            y, d = gelu_and_derivative(dot(w1t[...], e[m, :, sl]))
            act[m, :, sl] = y.astype(BF16)
            dg[m, :, sl] = d
            fc = dot(w2t[...], act[m, :, sl])
            for r in range(2):
                for l in range(4):
                    fs[q, r * 4 + l, m] = fc[64 * r : 64 * r + VH, 128 * l : 128 * l + 128]

        send_all("f", q, FORECAST)

    coef = (1.0 - (1.0 - ALPHA_FAIR) / TOTAL_MEM) / (TOTAL_MEM - 1)
    d2 = SMOOTH_WIDTH * SMOOTH_WIDTH

    def pairwise(q):
        mine_r, mine_l = me // 4, me % 4
        lanes = ds(q * CQ + mine_l * 128, 128, 128)
        mean = jnp.sum(jnp.sum(av[...], axis=0), keepdims=True) / TOTAL_CELLS
        area = aw[pl.ds(q * 4 + mine_l, 1), :] / mean

        def tile(rows, n):
            scale = area * vcol[mine_r, rows, :]
            t = tgt[mine_r, rows, lanes]
            f = [fr[q, k // 2, k % 2, rows, :] for k in range(TOTAL_MEM)]
            s = [None] * TOTAL_MEM
            spread = None
            for i in range(TOTAL_MEM):
                for k in range(i + 1, TOTAL_MEM):
                    d = f[i] - f[k]
                    w = d * d + d2
                    inv = lax.rsqrt(w)
                    slope = d * inv
                    s[i] = slope if s[i] is None else s[i] + slope
                    s[k] = -slope if s[k] is None else s[k] - slope
                    smooth = w * inv - SMOOTH_WIDTH
                    spread = smooth if spread is None else spread + smooth
            truth = None
            for i in range(TOTAL_MEM):
                d = f[i] - t
                w = d * d + d2
                inv = lax.rsqrt(w)
                gs[q, i // 2, i % 2, rows, :] = scale * (d * inv - coef * s[i])
                smooth = w * inv - SMOOTH_WIDTH
                truth = smooth if truth is None else truth + smooth
            loss[0:n, :] += scale * (truth / TOTAL_MEM - (coef / TOTAL_MEM) * spread)

        @pl.loop(0, VH // 8)
        def _(i):
            tile(ds(i * 8, 8, 8), 8)

        tile(pl.ds(VH // 8 * 8, VH % 8), VH % 8)
        send_all("g", q, BACK)

    def backward(q):
        sl = pl.ds(q * CQ, CQ)
        zeros = jnp.zeros((64 - VH, 128), F32)

        @pl.loop(0, MEM)
        def _(m):
            for r in range(2):
                for l in range(4):
                    block = jnp.concatenate([gr[q, r * 4 + l, m], zeros], axis=0)
                    gv[m, 64 * r : 64 * r + 64, q * CQ + 128 * l : q * CQ + 128 * l + 128] = (
                        block.astype(BF16)
                    )
            gp[m, :, sl] = (dot(w2p[...], gv[m, :, sl]) * dg[m, :, sl]).astype(BF16)

    def weight_gradients(q, half):
        sl = pl.ds(q * CQ, CQ)
        rows = ds(half * HALF, HALF, HALF)

        @pl.loop(0, 4)
        def _(j):
            cols = ds(j * 256, 256, 256)
            new = dot_t(e[0, rows, sl], gp[0, cols, sl]) + dot_t(e[1, rows, sl], gp[1, cols, sl])
            if q == 0:
                grad[rows, cols] = new
            else:
                grad[rows, cols] += new

        new = dot_t(act[0, rows, sl], gv[0, :, sl]) + dot_t(act[1, rows, sl], gv[1, :, sl])
        if q == 0:
            grad[rows, H:WIDE] = new
        else:
            grad[rows, H:WIDE] += new

    def embedding_derivative(m, q):
        sl = pl.ds(q * CQ, CQ)
        ed[m, :, sl] = dot(w1[...], gp[m, :, sl]).astype(BF16)

    def part_cols(p):
        return pl.ds(p * PW, PW)

    def along(p, level, s):
        return (pos[ORDERS[p][level]] + s) % 4

    def peer(p, level, s):
        return device(moved(**{ORDERS[p][level]: s}))

    def core_copy(s, p):
        k = along(p, 0, s)
        return remote(
            grad.at[ds((1 - core) * HALF + k * 128, 128, 128), part_cols(p)],
            core_in.at[ds(k * 128, 128, 128), part_cols(p)],
            core_s.at[s, p], core_r.at[s, p], device(moved(c=1)),
        )

    def block_rows(ks):
        begin = core * HALF
        for k, size in zip(ks, (128, 32, 8)):
            begin = begin + k * size
        size = (128, 32, 8)[len(ks) - 1]
        return ds(begin, size, size)

    def rs(level, p, s):
        k = along(p, level, s)
        src = (
            grad.at[block_rows([k]), part_cols(p)] if level == 0
            else r1.at[p, ds(k * 32, 32, 32)] if level == 1
            else r2.at[p, ds(k * 8, 8, 8)]
        )
        return remote(
            src, (s1, s2, s3)[level].at[p, s - 1],
            rs_s.at[level, p, s], rs_r.at[level, p, s], peer(p, level, s),
        )

    def ag(level, p, s, arriving):
        ks = [pos[a] for a in ORDERS[p][: level + 1]]
        if arriving:
            ks[level] = (ks[level] + 4 - s) % 4
        at = full.at[block_rows(ks), part_cols(p)]
        return remote(at, at, ag_s.at[level, p, s], ag_r.at[level, p, s], peer(p, level, s))

    def core_gather(p, s, c):
        k = along(p, 0, 4 - s)
        at = full.at[ds(c * HALF + k * 128, 128, 128), part_cols(p)]
        return remote(at, at, cg_s.at[p, s], cg_r.at[p, s], device(moved(c=1)))

    steps = OFFSETS + (0,)
    rescale = 1.0 / math.sqrt(TOTAL_MEM * TOTAL_CELLS)

    def run():
        begin()
        forward(0)
        forward(1)
        for o in range(1, 16):
            arrived(("area", o), area_arrival(o))
        receive_all("f", 0, FORECAST)
        pairwise(0)
        receive_all("f", 1, FORECAST)
        pairwise(1)
        receive_all("g", 0, BACK)
        backward(0)
        weight_gradients(0, 0)
        weight_gradients(0, 1)
        receive_all("g", 1, BACK)
        backward(1)
        weight_gradients(1, 1 - core)
        own_loss = jnp.sum(loss[...], keepdims=True)
        row = lax.broadcasted_iota(jnp.int32, (8, VP), 0)
        col = lax.broadcasted_iota(jnp.int32, (8, VP), 1)
        grad[0:8, H:WIDE] += jnp.where((row == 0) & (col == LOSS_COL), own_loss, 0.0)
        for s in steps:
            for p in range(3):
                start(("core", p, s), core_copy(s, p))
        weight_gradients(1, core)
        tiles = [(0, 0), (1, 0), (0, 1), (1, 1)]
        for n, s in enumerate(steps):
            for p in range(3):
                arrived(("core", p, s), core_copy(s, p))
                k = along(p, 0, s)
                rows, cols = block_rows([k]), part_cols(p)
                grad[rows, cols] += core_in[ds(k * 128, 128, 128), cols]
                if s:
                    start(("rs", 0, p, s), rs(0, p, s))
            embedding_derivative(*tiles[n])
        for p in range(3):
            for s in OFFSETS:
                arrived(("rs", 0, p, s), rs(0, p, s))
            rows = block_rows([along(p, 0, 0)])
            r1[p] = grad[rows, part_cols(p)] + s1[p, 0] + s1[p, 1] + s1[p, 2]
            for s in OFFSETS:
                start(("rs", 1, p, s), rs(1, p, s))
        for p in range(3):
            for s in OFFSETS:
                arrived(("rs", 1, p, s), rs(1, p, s))
            k = along(p, 1, 0)
            r2[p] = r1[p, ds(k * 32, 32, 32)] + s2[p, 0] + s2[p, 1] + s2[p, 2]
            for s in OFFSETS:
                start(("rs", 2, p, s), rs(2, p, s))
        for p in range(3):
            for s in OFFSETS:
                arrived(("rs", 2, p, s), rs(2, p, s))
            ks = [pos[a] for a in ORDERS[p]]
            total = r2[p, ds(ks[2] * 8, 8, 8)] + s3[p, 0] + s3[p, 1] + s3[p, 2]
            full[block_rows(ks), part_cols(p)] = total * rescale
            for s in OFFSETS:
                start(("ag", 2, p, s), ag(2, p, s, False))
        for level in (2, 1):
            for p in range(3):
                for s in OFFSETS:
                    arrived(("ag", level, p, s), ag(level, p, s, True))
                for s in OFFSETS:
                    start(("ag", level - 1, p, s), ag(level - 1, p, s, False))
                if level == 1:
                    start(("cg", p, 0), core_gather(p, 0, core))
        for s in (1, 3, 2):
            for p in range(3):
                arrived(("ag", 0, p, s), ag(0, p, s, True))
                start(("cg", p, s), core_gather(p, s, core))
        for s in (0, 1, 3, 2):
            for p in range(3):
                arrived(("cg", p, s), core_gather(p, s, 1 - core))

    run()
    for copy in sent.values():
        copy.wait_send()


def finish(ed, full, ed_out, grad_out, grad_t_out, penalty, sem):
    ed_copy = pltpu.make_async_copy(ed, ed_out, sem.at[0])
    ed_copy.start()
    grad_copy = pltpu.make_async_copy(full.at[:, 0:H], grad_out, sem.at[1])
    grad_copy.start()
    t = full[:, H:WIDE].T
    grad_t_out[0:VH] = t[0:VH]
    grad_t_out[VH:V] = t[64 : 64 + VH]
    rescale = 1.0 / math.sqrt(TOTAL_MEM * TOTAL_CELLS)
    at = full[0:1, H + LOSS_COL : H + LOSS_COL + 1]
    penalty[...] = at * (1.0 / (rescale * TOTAL_CELLS * V))
    ed_copy.wait()
    grad_copy.wait()


def per_device(
    embedding_tensor,
    first_projection_matrix,
    variable_projection_matrix,
    target,
    var_weight,
    area_weight,
):
    vmem = pl.BlockSpec(memory_space=pltpu.VMEM)
    hbm = pl.BlockSpec(memory_space=pl.ANY)
    dma = pltpu.SemaphoreType.DMA
    big = (MEM, H, CELLS)
    swap = (NQ, 8, MEM, VH, 128)
    in_vmem = (pltpu.VMEM(big, BF16), pltpu.VMEM((H, WIDE), F32))
    ed, full = pl.pallas_call(
        kernel,
        name="decoder_crps",
        out_shape=in_vmem,
        in_specs=[hbm, hbm, vmem, vmem, vmem, vmem],
        out_specs=(vmem, vmem),
        scratch_shapes=[
            pltpu.VMEM(big, BF16),
            pltpu.VMEM((H, H), BF16),
            pltpu.VMEM((H, H), BF16),
            pltpu.VMEM((H, VP), BF16),
            pltpu.VMEM((VP, H), BF16),
            pltpu.VMEM(big, BF16),
            pltpu.VMEM(big, F32),
            pltpu.VMEM((MEM, VP, CELLS), BF16),
            pltpu.VMEM(big, BF16),
            pltpu.VMEM((2, VH, CELLS), F32),
            pltpu.VMEM((2, VH, 128), F32),
            pltpu.VMEM((16, 8, 128), F32),
            pltpu.VMEM(swap, F32),
            pltpu.VMEM(swap, F32),
            pltpu.VMEM(swap, F32),
            pltpu.VMEM(swap, F32),
            pltpu.VMEM((H, WIDE), F32),
            pltpu.VMEM((HALF, WIDE), F32),
            pltpu.VMEM((3, 3, 128, PW), F32),
            pltpu.VMEM((3, 128, PW), F32),
            pltpu.VMEM((3, 3, 32, PW), F32),
            pltpu.VMEM((3, 32, PW), F32),
            pltpu.VMEM((3, 3, 8, PW), F32),
            pltpu.VMEM((8, 128), F32),
            dma((5,)),
            dma((16,)), dma((16,)),
            dma((NQ, 8)), dma((NQ, 8)),
            dma((NQ, 8)), dma((NQ, 8)),
            dma((4, 3)), dma((4, 3)),
            dma((3, 3, 4)), dma((3, 3, 4)),
            dma((3, 3, 4)), dma((3, 3, 4)),
            dma((3, 4)), dma((3, 4)),
        ],
        compiler_params=pltpu.CompilerParams(
            collective_id=0, has_side_effects=True, vmem_limit_bytes=50 * 2**20
        ),
        cost_estimate=pl.CostEstimate(
            flops=15_000_000_000, bytes_accessed=20_000_000, transcendentals=4_000_000
        ),
    )(
        embedding_tensor,
        first_projection_matrix,
        variable_projection_matrix.T,
        target,
        var_weight.reshape(1, V),
        area_weight.reshape(8, 128),
    )
    ed, grad_in, grad_out_t, penalty = pl.pallas_call(
        finish,
        name="write_out",
        out_shape=(
            jax.ShapeDtypeStruct(big, BF16),
            jax.ShapeDtypeStruct((H, H), F32),
            jax.ShapeDtypeStruct((V, H), F32),
            jax.ShapeDtypeStruct((1, 1), F32),
        ),
        in_specs=[vmem, vmem],
        out_specs=(hbm, hbm, vmem, vmem),
        scratch_shapes=[dma((2,))],
        compiler_params=pltpu.CompilerParams(vmem_limit_bytes=8 * 2**20),
    )(ed, full)
    return ed, grad_in, grad_out_t.T, penalty[0, 0]


def solution(mesh):
    in_specs = (P("member", None, "grid"), P(), P(), P(None, "grid"), P(), P("grid"))
    out_specs = (P("member", None, "grid"), P(), P(), P())
    return jax.shard_map(
        per_device, mesh=mesh, in_specs=in_specs, out_specs=out_specs, check_vma=False
    )
```

```python
import functools
import math

import jax
import jax.numpy as jnp
from jax import lax
from jax.experimental import pallas as pl
from jax.experimental.pallas import tpu as pltpu
from jax.sharding import PartitionSpec as P

SMOOTH_WIDTH = 0.1
ALPHA_FAIR = 0.95
MESH = pl.DeviceIdType.MESH
F32 = jnp.float32
BF16 = jnp.bfloat16
GELU_A = math.sqrt(2.0 / math.pi)
GELU_B = 0.044715

H = 1024
V = 100
CELLS = 1024
MEM = 2
TOTAL_MEM = 16
TOTAL_CELLS = 16384
NQ = 4
CQ = CELLS // NQ
NL = CQ // 128
NR = 8 // NL
VH = V // NR
VG = 128 // NR
VP = NR * VG
HALF = H // 2
WIDE = H + VP
NU = WIDE // 128
LOSS_COL = VH
ORDERS = (("x", "y", "z"), ("y", "z", "x"), ("z", "x", "y"))
OFFSETS = (2, 1, 3)


def dot(a, b):
    return lax.dot_general(a, b, (((1,), (0,)), ((), ())), preferred_element_type=F32)


def dot_t(a, b):
    return lax.dot_general(a, b, (((1,), (1,)), ((), ())), preferred_element_type=F32)


def gelu_and_derivative(x):
    x2 = x * x
    t = jnp.tanh(x * (GELU_A + (GELU_A * GELU_B) * x2))
    h = 0.5 + 0.5 * t
    y = x * h
    return y, h + (y * (1.0 - t)) * (GELU_A + (3.0 * GELU_A * GELU_B) * x2)


def ds(start, size, multiple):
    return pl.ds(pl.multiple_of(start, multiple), size)


def kernel(
    emb, w1_hbm, w2_hbm, target_hbm, vw_hbm, aw_hbm,
    ed, full,
    e, w1, w1t, w2_in, target, vw, aw, w2p, w2t, act, dg, gv, gp, tgt, vcol, av,
    fs, fr, gs, gr, grad, core_in, s1, r1, s2, s3, loss,
    in_sem, area_sem, f_sem, g_sem, core_sem, rs0_sem, rs1_sem, x_sem, ag1_sem, ag0_sem, cg_sem,
):
    me = lax.axis_index("member")
    g = lax.axis_index("grid")
    pos = {"x": me % 4, "y": (g // 8) * 2 + me // 4, "z": (g // 2) % 4, "c": g % 2}
    core = pos["c"]

    def device(p):
        return ((p["y"] % 2) * 4 + p["x"], ((p["y"] // 2) * 4 + p["z"]) * 2 + p["c"])

    def moved(**by):
        return {k: (v + by[k]) % (2 if k == "c" else 4) if k in by else v for k, v in pos.items()}

    def remote(src, dst, send_sem, recv_sem, to):
        return pltpu.make_async_remote_copy(
            src_ref=src, dst_ref=dst, send_sem=send_sem, recv_sem=recv_sem,
            device_id=to, device_id_type=MESH,
        )

    other_core = device(moved(c=1))

    def arrived(ref, sem):
        remote(ref, ref, sem, sem, other_core).wait_recv()

    def left(ref, sem):
        remote(ref, ref, sem, sem, other_core).wait_send()

    def member_peer(o):
        return (me // 4 + o // 4) % 2 * 4 + (me % 4 + o % 4) % 4

    def emb_copy(q):
        sl = pl.ds(q * CQ, CQ)
        return pltpu.make_async_copy(emb.at[:, :, sl], e.at[:, :, sl], in_sem.at[q])

    w1_copy = pltpu.make_async_copy(w1_hbm, w1, in_sem.at[NQ])
    small_copies = [
        pltpu.make_async_copy(src, dst, in_sem.at[NQ + 1 + i])
        for i, (src, dst) in enumerate(
            ((w2_hbm, w2_in), (target_hbm, target), (vw_hbm, vw), (aw_hbm, aw))
        )
    ]
    barrier = pltpu.get_barrier_semaphore()

    def load():
        w1_copy.start()
        for copy in small_copies:
            copy.start()
        for q in range(NQ):
            emb_copy(q).start()

    def greet():
        peers = [(member_peer(o), g) for o in range(1, 8)]
        peers += [(me, (g + o) % 16) for o in range(1, 16)]
        peers += [((me + 4) % 8, (g + 8) % 16)]
        for peer in peers:
            pl.semaphore_signal(barrier, inc=1, device_id=peer, device_id_type=MESH)

    def small_operands():
        for copy in small_copies:
            copy.wait()
        wide = w2_in[...].astype(F32)
        gap = jnp.zeros((VG - VH, H), F32)
        groups = []
        for r in range(NR):
            groups += [wide[r * VH : r * VH + VH], gap]
        w2t[...] = jnp.concatenate(groups, axis=0).astype(BF16)
        w2p[...] = w2t[...].T
        t32 = target[...].astype(F32)
        columns = jnp.broadcast_to(vw[...], (128, V)).T
        for r in range(NR):
            tgt[r] = t32[r * VH : r * VH + VH]
            vcol[r] = columns[r * VH : r * VH + VH]
        av[g] = aw[...]
        loss[...] = jnp.zeros_like(loss)

    def send_area():
        for o in range(1, 16):
            remote(
                av.at[g], av.at[g], area_sem.at[0], area_sem.at[1], (me, (g + o) % 16)
            ).start()

    PEERS = (6, 2, 5, 7, 4, 1, 3)

    def send_all(q, src, dst, sem):
        for o in PEERS:
            peer = member_peer(o)
            remote(src.at[q, peer], dst.at[q, me], sem.at[NQ], sem.at[q], (peer, g)).start()
        dst[q, me] = src[q, me]

    def receive_all(q, dst, sem):
        arrived(dst.at[q, pl.ds(0, 7)], sem.at[q])

    def forward(q):
        sl = pl.ds(q * CQ, CQ)
        emb_copy(q).wait()

        @pl.loop(0, MEM)
        def _(m):
            y, d = gelu_and_derivative(dot(w1t[...], e[m, :, sl]))
            act[m, :, sl] = y.astype(BF16)
            dg[m, :, sl] = d
            fc = dot(w2t[...], act[m, :, sl])
            for r in range(NR):
                for l in range(NL):
                    fs[q, r * NL + l, m] = fc[VG * r : VG * r + VH, 128 * l : 128 * l + 128]

    coef = (1.0 - (1.0 - ALPHA_FAIR) / TOTAL_MEM) / (TOTAL_MEM - 1)
    d2 = SMOOTH_WIDTH * SMOOTH_WIDTH

    def pairwise(q):
        mine_r, mine_l = me // NL, me % NL
        lanes = ds(q * CQ + mine_l * 128, 128, 128)
        mean = jnp.sum(jnp.sum(av[...], axis=0), keepdims=True) / TOTAL_CELLS
        area = aw[pl.ds(q * NL + mine_l, 1), :] / mean

        def tile(rows, n):
            scale = area * vcol[mine_r, rows, :]
            t = tgt[mine_r, rows, lanes]
            f = [fr[q, k // 2, k % 2, rows, :] for k in range(TOTAL_MEM)]
            s = [None] * TOTAL_MEM
            spread = None
            for i in range(TOTAL_MEM):
                for k in range(i + 1, TOTAL_MEM):
                    d = f[i] - f[k]
                    w = d * d + d2
                    inv = lax.rsqrt(w)
                    slope = d * inv
                    s[i] = slope if s[i] is None else s[i] + slope
                    s[k] = -slope if s[k] is None else s[k] - slope
                    smooth = w * inv - SMOOTH_WIDTH
                    spread = smooth if spread is None else spread + smooth
            truth = None
            for i in range(TOTAL_MEM):
                d = f[i] - t
                w = d * d + d2
                inv = lax.rsqrt(w)
                gs[q, i // 2, i % 2, rows, :] = scale * (d * inv - coef * s[i])
                smooth = w * inv - SMOOTH_WIDTH
                truth = smooth if truth is None else truth + smooth
            loss[0:n, :] += scale * (truth / TOTAL_MEM - (coef / TOTAL_MEM) * spread)

        @pl.loop(0, VH // 8)
        def _(i):
            tile(ds(i * 8, 8, 8), 8)

        tile(pl.ds(VH // 8 * 8, VH % 8), VH % 8)

    def backward(q):
        sl = pl.ds(q * CQ, CQ)
        gap = jnp.zeros((VG - VH, 128), F32)

        @pl.loop(0, MEM)
        def _(m):
            for l in range(NL):
                groups = []
                for r in range(NR):
                    groups += [gr[q, r * NL + l, m], gap]
                at = q * CQ + 128 * l
                gv[m, :, at : at + 128] = jnp.concatenate(groups, axis=0).astype(BF16)
            gp[m, :, sl] = (dot(w2p[...], gv[m, :, sl]) * dg[m, :, sl]).astype(BF16)

    def add_to_grad(rows, cols, new, first):
        if first:
            grad[rows, cols] = new
        else:
            grad[rows, cols] += new

    def grad_in_tile(sl, half, j, first):
        rows, cols = ds(half * HALF, HALF, HALF), ds(j * 256, 256, 256)
        new = dot_t(e[0, rows, sl], gp[0, cols, sl]) + dot_t(e[1, rows, sl], gp[1, cols, sl])
        add_to_grad(rows, cols, new, first)

    def grad_out_tile(sl, half, first):
        rows = ds(half * HALF, HALF, HALF)
        new = dot_t(act[0, rows, sl], gv[0, :, sl]) + dot_t(act[1, rows, sl], gv[1, :, sl])
        add_to_grad(rows, pl.ds(H, VP), new, first)

    def weight_gradients(q, n, half):
        sl = pl.ds(q * CQ, n * CQ)

        @pl.loop(0, 4)
        def _(j):
            grad_in_tile(sl, half, j, q == 0)

        grad_out_tile(sl, half, q == 0)

    def embedding_derivative(m, q):
        sl = pl.ds(q * 512, 512)
        ed[m, :, sl] = dot(w1[...], gp[m, :, sl]).astype(BF16)

    def cols_of(u):
        return pl.ds(u * 128, 128)

    def along(u, level, s):
        return (pos[ORDERS[u % 3][level]] + s) % 4

    def peer_of(u, level, s):
        return device(moved(**{ORDERS[u % 3][level]: s}))

    def block_rows(ks):
        begin = core * HALF
        for k, size in zip(ks, (128, 32)):
            begin = begin + k * size
        size = (128, 32)[len(ks) - 1]
        return ds(begin, size, size)

    def core_send(u):
        remote(
            grad.at[ds((1 - core) * HALF, HALF, HALF), cols_of(u)], core_in.at[:, cols_of(u)],
            core_sem.at[NU], core_sem.at[u], other_core,
        ).start()

    def core_receive(u):
        cols = cols_of(u)
        arrived(core_in.at[:, cols], core_sem.at[u])
        grad[ds(core * HALF, HALF, HALF), cols] += core_in[:, cols]
        for s in OFFSETS:
            k = along(u, 0, s)
            remote(
                grad.at[block_rows([k]), cols], s1.at[u, s - 1],
                rs0_sem.at[NU], rs0_sem.at[u], peer_of(u, 0, s),
            ).start()

    def rs0_receive(u):
        arrived(s1.at[u], rs0_sem.at[u])
        own = grad[block_rows([along(u, 0, 0)]), cols_of(u)]
        r1[u] = own + s1[u, 0] + s1[u, 1] + s1[u, 2]
        for s in OFFSETS:
            k = along(u, 1, s)
            remote(
                r1.at[u, ds(k * 32, 32, 32)], s2.at[u, s - 1],
                rs1_sem.at[NU], rs1_sem.at[u], peer_of(u, 1, s),
            ).start()

    def rs1_receive(u):
        arrived(s2.at[u], rs1_sem.at[u])
        own = r1[u, ds(along(u, 1, 0) * 32, 32, 32)]
        k = along(u, 2, 0)
        s3[u, k] = own + s2[u, 0] + s2[u, 1] + s2[u, 2]
        for s in OFFSETS:
            remote(
                s3.at[u, k], s3.at[u, k], x_sem.at[NU], x_sem.at[u], peer_of(u, 2, s)
            ).start()

    rescale = 1.0 / math.sqrt(TOTAL_MEM * TOTAL_CELLS)

    def x_receive(u):
        arrived(s3.at[u, pl.ds(0, 3)], x_sem.at[u])
        at = (block_rows([along(u, 0, 0), along(u, 1, 0)]), cols_of(u))
        full[at] = (s3[u, 0] + s3[u, 1] + s3[u, 2] + s3[u, 3]) * rescale
        for s in OFFSETS:
            remote(
                full.at[at], full.at[at], ag1_sem.at[NU], ag1_sem.at[u], peer_of(u, 1, s)
            ).start()

    def to_core(u, s):
        at = (block_rows([along(u, 0, s)]), cols_of(u))
        remote(full.at[at], full.at[at], cg_sem.at[NU], cg_sem.at[u], other_core).start()

    def ag1_receive(u):
        arrived(full.at[pl.ds(0, 96), cols_of(u)], ag1_sem.at[u])
        at = (block_rows([along(u, 0, 0)]), cols_of(u))
        for s in OFFSETS:
            remote(
                full.at[at], full.at[at], ag0_sem.at[NU], ag0_sem.at[u], peer_of(u, 0, s)
            ).start()
        to_core(u, 0)

    def ag0_receive(u):
        arrived(full.at[pl.ds(0, 384), cols_of(u)], ag0_sem.at[u])
        for s in OFFSETS:
            to_core(u, s)

    def cg_receive(u):
        arrived(full.at[pl.ds(0, HALF), cols_of(u)], cg_sem.at[u])

    def run():
        load()
        greet()
        small_operands()
        w1_copy.wait()
        w1t[...] = w1[...].T
        forward(0)
        pl.semaphore_wait(barrier, 23)
        send_area()
        send_all(0, fs, fr, f_sem)
        forward(1)
        send_all(1, fs, fr, f_sem)
        forward(2)
        send_all(2, fs, fr, f_sem)
        arrived(av.at[pl.ds(0, 15)], area_sem.at[1])
        receive_all(0, fr, f_sem)
        pairwise(0)
        send_all(0, gs, gr, g_sem)
        forward(3)
        send_all(3, fs, fr, f_sem)
        receive_all(1, fr, f_sem)
        pairwise(1)
        send_all(1, gs, gr, g_sem)
        receive_all(2, fr, f_sem)
        pairwise(2)
        send_all(2, gs, gr, g_sem)
        receive_all(0, gr, g_sem)
        backward(0)
        receive_all(3, fr, f_sem)
        pairwise(3)
        send_all(3, gs, gr, g_sem)
        receive_all(1, gr, g_sem)
        backward(1)
        weight_gradients(0, 2, 0)
        weight_gradients(0, 2, 1)
        receive_all(2, gr, g_sem)
        backward(2)
        weight_gradients(2, 1, 0)
        weight_gradients(2, 1, 1)
        receive_all(3, gr, g_sem)
        backward(3)
        own_loss = jnp.sum(loss[...], keepdims=True)
        row = lax.broadcasted_iota(jnp.int32, (8, VP), 0)
        col = lax.broadcasted_iota(jnp.int32, (8, VP), 1)
        grad[0:8, H:WIDE] += jnp.where((row == 0) & (col == LOSS_COL), own_loss, 0.0)
        last = pl.ds(3 * CQ, CQ)
        for j in range(4):
            grad_in_tile(last, 1 - core, j, False)
            core_send(2 * j)
            core_send(2 * j + 1)
        grad_out_tile(last, 1 - core, False)
        core_send(NU - 1)
        weight_gradients(3, 1, core)
        waves = ((0, 1, 2), (3, 4, 5), (6, 7, 8))

        def each(step, wave):
            for u in waves[wave]:
                step(u)

        each(core_receive, 0)
        embedding_derivative(0, 0)
        each(core_receive, 1)
        embedding_derivative(1, 0)
        each(core_receive, 2)
        each(rs0_receive, 0)
        embedding_derivative(0, 1)
        each(rs0_receive, 1)
        each(rs1_receive, 0)
        embedding_derivative(1, 1)
        each(rs0_receive, 2)
        each(rs1_receive, 1)
        each(x_receive, 0)
        each(rs1_receive, 2)
        each(x_receive, 1)
        each(ag1_receive, 0)
        each(x_receive, 2)
        each(ag1_receive, 1)
        each(ag1_receive, 2)
        each(ag0_receive, 0)
        each(ag0_receive, 1)
        each(ag0_receive, 2)
        for wave in range(3):
            each(cg_receive, wave)

    run()
    left(av.at[pl.ds(0, 15)], area_sem.at[0])
    left(fs.at[:, pl.ds(0, 7)], f_sem.at[NQ])
    left(gs.at[:, pl.ds(0, 7)], g_sem.at[NQ])
    left(core_in, core_sem.at[NU])
    left(s1, rs0_sem.at[NU])
    left(s2, rs1_sem.at[NU])
    left(s3.at[:, pl.ds(0, 3)], x_sem.at[NU])
    left(s2, ag1_sem.at[NU])
    left(s1, ag0_sem.at[NU])
    left(core_in, cg_sem.at[NU])


def finish(ed, full, ed_out, grad_out, grad_t_out, penalty, sem):
    ed_copy = pltpu.make_async_copy(ed, ed_out, sem.at[0])
    ed_copy.start()
    grad_copy = pltpu.make_async_copy(full.at[:, 0:H], grad_out, sem.at[1])
    grad_copy.start()
    t = full[:, H:WIDE].T
    grad_t_out[...] = jnp.concatenate([t[VG * r : VG * r + VH] for r in range(NR)], axis=0)
    rescale = 1.0 / math.sqrt(TOTAL_MEM * TOTAL_CELLS)
    at = full[0:1, H + LOSS_COL : H + LOSS_COL + 1]
    penalty[...] = at * (1.0 / (rescale * TOTAL_CELLS * V))
    ed_copy.wait()
    grad_copy.wait()


def per_device(
    embedding_tensor,
    first_projection_matrix,
    variable_projection_matrix,
    target,
    var_weight,
    area_weight,
):
    vmem = pl.BlockSpec(memory_space=pltpu.VMEM)
    hbm = pl.BlockSpec(memory_space=pl.ANY)
    dma = pltpu.SemaphoreType.DMA
    big = (MEM, H, CELLS)
    swap = (NQ, 8, MEM, VH, 128)
    in_vmem = (pltpu.VMEM(big, BF16), pltpu.VMEM((H, WIDE), F32))
    ed, full = pl.pallas_call(
        kernel,
        name="decoder_crps",
        out_shape=in_vmem,
        in_specs=[hbm] * 6,
        out_specs=(vmem, vmem),
        scratch_shapes=[
            pltpu.VMEM(big, BF16),
            pltpu.VMEM((H, H), BF16),
            pltpu.VMEM((H, H), BF16),
            pltpu.VMEM((V, H), BF16),
            pltpu.VMEM((V, CELLS), BF16),
            pltpu.VMEM((1, V), F32),
            pltpu.VMEM((8, 128), F32),
            pltpu.VMEM((H, VP), BF16),
            pltpu.VMEM((VP, H), BF16),
            pltpu.VMEM(big, BF16),
            pltpu.VMEM(big, F32),
            pltpu.VMEM((MEM, VP, CELLS), BF16),
            pltpu.VMEM(big, BF16),
            pltpu.VMEM((NR, VH, CELLS), F32),
            pltpu.VMEM((NR, VH, 128), F32),
            pltpu.VMEM((16, 8, 128), F32),
            pltpu.VMEM(swap, F32),
            pltpu.VMEM(swap, F32),
            pltpu.VMEM(swap, F32),
            pltpu.VMEM(swap, F32),
            pltpu.VMEM((H, WIDE), F32),
            pltpu.VMEM((HALF, WIDE), F32),
            pltpu.VMEM((NU, 3, 128, 128), F32),
            pltpu.VMEM((NU, 128, 128), F32),
            pltpu.VMEM((NU, 3, 32, 128), F32),
            pltpu.VMEM((NU, 4, 32, 128), F32),
            pltpu.VMEM((8, 128), F32),
            dma((NQ + 5,)),
            dma((2,)),
            dma((NQ + 1,)), dma((NQ + 1,)),
            dma((NU + 1,)), dma((NU + 1,)), dma((NU + 1,)), dma((NU + 1,)),
            dma((NU + 1,)), dma((NU + 1,)), dma((NU + 1,)),
        ],
        compiler_params=pltpu.CompilerParams(
            collective_id=0, has_side_effects=True, vmem_limit_bytes=50 * 2**20
        ),
        cost_estimate=pl.CostEstimate(
            flops=15_000_000_000, bytes_accessed=20_000_000, transcendentals=4_000_000
        ),
    )(
        embedding_tensor,
        first_projection_matrix,
        variable_projection_matrix.T,
        target,
        var_weight.reshape(1, V),
        area_weight.reshape(8, 128),
    )
    ed, grad_in, grad_out_t, penalty = pl.pallas_call(
        finish,
        name="write_out",
        out_shape=(
            jax.ShapeDtypeStruct(big, BF16),
            jax.ShapeDtypeStruct((H, H), F32),
            jax.ShapeDtypeStruct((V, H), F32),
            jax.ShapeDtypeStruct((1, 1), F32),
        ),
        in_specs=[vmem, vmem],
        out_specs=(hbm, hbm, vmem, vmem),
        scratch_shapes=[dma((2,))],
        compiler_params=pltpu.CompilerParams(vmem_limit_bytes=8 * 2**20),
    )(ed, full)
    return ed, grad_in, grad_out_t.T, penalty[0, 0]


def solution(mesh):
    in_specs = (P("member", None, "grid"), P(), P(), P(None, "grid"), P(), P("grid"))
    out_specs = (P("member", None, "grid"), P(), P(), P())
    return jax.shard_map(
        per_device, mesh=mesh, in_specs=in_specs, out_specs=out_specs, check_vma=False
    )
```

```python
import functools
import math

import jax
import jax.numpy as jnp
from jax import lax
from jax.experimental import pallas as pl
from jax.experimental.pallas import tpu as pltpu
from jax.sharding import PartitionSpec as P

SMOOTH_WIDTH = 0.1
ALPHA_FAIR = 0.95
MESH = pl.DeviceIdType.MESH
F32 = jnp.float32
BF16 = jnp.bfloat16
GELU_A = math.sqrt(2.0 / math.pi)
GELU_B = 0.044715

H = 1024
V = 100
CELLS = 1024
MEM = 2
TOTAL_MEM = 16
TOTAL_CELLS = 16384
NQ = 4
CQ = CELLS // NQ
NL = CQ // 128
NR = 8 // NL
VH = V // NR
VG = 128 // NR
VP = NR * VG
HALF = H // 2
WIDE = H + VP
NU = WIDE // 128
LOSS_COL = VH
ORDERS = (("x", "y", "z"), ("y", "z", "x"), ("z", "x", "y"))
OFFSETS = (2, 1, 3)


def dot(a, b):
    return lax.dot_general(a, b, (((1,), (0,)), ((), ())), preferred_element_type=F32)


def dot_t(a, b):
    return lax.dot_general(a, b, (((1,), (1,)), ((), ())), preferred_element_type=F32)


def gelu_and_derivative(x):
    x2 = x * x
    t = jnp.tanh(x * (GELU_A + (GELU_A * GELU_B) * x2))
    h = 0.5 + 0.5 * t
    y = x * h
    return y, h + (y * (1.0 - t)) * (GELU_A + (3.0 * GELU_A * GELU_B) * x2)


def ds(start, size, multiple):
    return pl.ds(pl.multiple_of(start, multiple), size)


def kernel(
    emb, w1_hbm, w2_hbm, target_hbm, vw_hbm, aw_hbm,
    ed, full,
    e, w1, w1t, w2_in, target, vw, aw, w2p, w2t, act, dg, gv, gp, tgt, vcol, av,
    fs, fr, gs, gr, grad, core_in, s1, r1, s2, s3, loss,
    in_sem, area_sem, f_sem, g_sem, core_sem, rs0_sem, rs1_sem, x_sem, ag1_sem, ag0_sem, cg_sem,
):
    me = lax.axis_index("member")
    g = lax.axis_index("grid")
    pos = {"x": me % 4, "y": (g // 8) * 2 + me // 4, "z": (g // 2) % 4, "c": g % 2}
    core = pos["c"]

    def device(p):
        return ((p["y"] % 2) * 4 + p["x"], ((p["y"] // 2) * 4 + p["z"]) * 2 + p["c"])

    def moved(**by):
        return {k: (v + by[k]) % (2 if k == "c" else 4) if k in by else v for k, v in pos.items()}

    def remote(src, dst, send_sem, recv_sem, to):
        return pltpu.make_async_remote_copy(
            src_ref=src, dst_ref=dst, send_sem=send_sem, recv_sem=recv_sem,
            device_id=to, device_id_type=MESH,
        )

    other_core = device(moved(c=1))

    def arrived(ref, sem):
        remote(ref, ref, sem, sem, other_core).wait_recv()

    def left(ref, sem):
        remote(ref, ref, sem, sem, other_core).wait_send()

    def member_peer(o):
        return (me // 4 + o // 4) % 2 * 4 + (me % 4 + o % 4) % 4

    def emb_copy(q):
        sl = pl.ds(q * CQ, CQ)
        return pltpu.make_async_copy(emb.at[:, :, sl], e.at[:, :, sl], in_sem.at[q])

    w1_copy = pltpu.make_async_copy(w1_hbm, w1, in_sem.at[NQ])
    small_copies = [
        pltpu.make_async_copy(src, dst, in_sem.at[NQ + 1 + i])
        for i, (src, dst) in enumerate(
            ((w2_hbm, w2_in), (target_hbm, target), (vw_hbm, vw), (aw_hbm, aw))
        )
    ]
    barrier = pltpu.get_barrier_semaphore()

    def load():
        w1_copy.start()
        for copy in small_copies:
            copy.start()
        for q in range(NQ):
            emb_copy(q).start()

    def greet():
        peers = [(member_peer(o), g) for o in range(1, 8)]
        peers += [(me, (g + o) % 16) for o in range(1, 16)]
        peers += [((me + 4) % 8, (g + 8) % 16)]
        for peer in peers:
            pl.semaphore_signal(barrier, inc=1, device_id=peer, device_id_type=MESH)

    def small_operands():
        for copy in small_copies:
            copy.wait()
        wide = w2_in[...].astype(F32)
        gap = jnp.zeros((VG - VH, H), F32)
        groups = []
        for r in range(NR):
            groups += [wide[r * VH : r * VH + VH], gap]
        w2t[...] = jnp.concatenate(groups, axis=0).astype(BF16)
        w2p[...] = w2t[...].T
        t32 = target[...].astype(F32)
        columns = jnp.broadcast_to(vw[...], (128, V)).T
        for r in range(NR):
            tgt[r] = t32[r * VH : r * VH + VH]
            vcol[r] = columns[r * VH : r * VH + VH]
        av[g] = aw[...]
        loss[...] = jnp.zeros_like(loss)

    def send_area():
        for o in range(1, 16):
            remote(
                av.at[g], av.at[g], area_sem.at[0], area_sem.at[1], (me, (g + o) % 16)
            ).start()

    PEERS = (6, 2, 5, 7, 4, 1, 3)

    def send_all(q, src, dst, sem):
        for o in PEERS:
            peer = member_peer(o)
            remote(src.at[q, peer], dst.at[q, me], sem.at[NQ], sem.at[q], (peer, g)).start()
        dst[q, me] = src[q, me]

    def receive_all(q, dst, sem):
        arrived(dst.at[q, pl.ds(0, 7)], sem.at[q])

    def forward(q):
        sl = pl.ds(q * CQ, CQ)
        emb_copy(q).wait()

        @pl.loop(0, MEM)
        def _(m):
            y, d = gelu_and_derivative(dot(w1t[...], e[m, :, sl]))
            act[m, :, sl] = y.astype(BF16)
            dg[m, :, sl] = d
            fc = dot(w2t[...], act[m, :, sl])
            for r in range(NR):
                for l in range(NL):
                    fs[q, r * NL + l, m] = fc[VG * r : VG * r + VH, 128 * l : 128 * l + 128]

    coef = (1.0 - (1.0 - ALPHA_FAIR) / TOTAL_MEM) / (TOTAL_MEM - 1)
    d2 = SMOOTH_WIDTH * SMOOTH_WIDTH

    def pairwise(q):
        mine_r, mine_l = me // NL, me % NL
        lanes = ds(q * CQ + mine_l * 128, 128, 128)
        mean = jnp.sum(jnp.sum(av[...], axis=0), keepdims=True) / TOTAL_CELLS
        area = aw[pl.ds(q * NL + mine_l, 1), :] / mean

        def tile(rows, n):
            scale = area * vcol[mine_r, rows, :]
            t = tgt[mine_r, rows, lanes]
            f = [fr[q, k // 2, k % 2, rows, :] for k in range(TOTAL_MEM)]
            s = [None] * TOTAL_MEM
            spread = None
            for i in range(TOTAL_MEM):
                for k in range(i + 1, TOTAL_MEM):
                    d = f[i] - f[k]
                    w = d * d + d2
                    inv = lax.rsqrt(w)
                    slope = d * inv
                    s[i] = slope if s[i] is None else s[i] + slope
                    s[k] = -slope if s[k] is None else s[k] - slope
                    smooth = w * inv - SMOOTH_WIDTH
                    spread = smooth if spread is None else spread + smooth
            truth = None
            for i in range(TOTAL_MEM):
                d = f[i] - t
                w = d * d + d2
                inv = lax.rsqrt(w)
                gs[q, i // 2, i % 2, rows, :] = scale * (d * inv - coef * s[i])
                smooth = w * inv - SMOOTH_WIDTH
                truth = smooth if truth is None else truth + smooth
            loss[0:n, :] += scale * (truth / TOTAL_MEM - (coef / TOTAL_MEM) * spread)

        @pl.loop(0, VH // 8)
        def _(i):
            tile(ds(i * 8, 8, 8), 8)

        tile(pl.ds(VH // 8 * 8, VH % 8), VH % 8)

    def backward(q):
        sl = pl.ds(q * CQ, CQ)
        gap = jnp.zeros((VG - VH, 128), F32)

        @pl.loop(0, MEM)
        def _(m):
            for l in range(NL):
                groups = []
                for r in range(NR):
                    groups += [gr[q, r * NL + l, m], gap]
                at = q * CQ + 128 * l
                gv[m, :, at : at + 128] = jnp.concatenate(groups, axis=0).astype(BF16)
            gp[m, :, sl] = (dot(w2p[...], gv[m, :, sl]) * dg[m, :, sl]).astype(BF16)

    def add_to_grad(rows, cols, new, first):
        if first:
            grad[rows, cols] = new
        else:
            grad[rows, cols] += new

    def grad_in_tile(sl, half, j, first):
        rows, cols = ds(half * HALF, HALF, HALF), ds(j * 256, 256, 256)
        new = dot_t(e[0, rows, sl], gp[0, cols, sl]) + dot_t(e[1, rows, sl], gp[1, cols, sl])
        add_to_grad(rows, cols, new, first)

    def grad_out_tile(sl, half, first):
        rows = ds(half * HALF, HALF, HALF)
        new = dot_t(act[0, rows, sl], gv[0, :, sl]) + dot_t(act[1, rows, sl], gv[1, :, sl])
        add_to_grad(rows, pl.ds(H, VP), new, first)

    def weight_gradients(q, n, half):
        sl = pl.ds(q * CQ, n * CQ)

        @pl.loop(0, 4)
        def _(j):
            grad_in_tile(sl, half, j, q == 0)

        grad_out_tile(sl, half, q == 0)

    def embedding_derivative(m, q):
        sl = pl.ds(q * 512, 512)
        ed[m, :, sl] = dot(w1[...], gp[m, :, sl]).astype(BF16)

    def cols_of(u):
        return pl.ds(u * 128, 128)

    def along(u, level, s):
        return (pos[ORDERS[u % 3][level]] + s) % 4

    def peer_of(u, level, s):
        return device(moved(**{ORDERS[u % 3][level]: s}))

    def block_rows(ks):
        begin = core * HALF
        for k, size in zip(ks, (128, 32)):
            begin = begin + k * size
        size = (128, 32)[len(ks) - 1]
        return ds(begin, size, size)

    def core_send(u):
        remote(
            grad.at[ds((1 - core) * HALF, HALF, HALF), cols_of(u)], core_in.at[:, cols_of(u)],
            core_sem.at[NU], core_sem.at[u], other_core,
        ).start()

    def core_receive(u):
        cols = cols_of(u)
        arrived(core_in.at[:, cols], core_sem.at[u])
        grad[ds(core * HALF, HALF, HALF), cols] += core_in[:, cols]
        for s in OFFSETS:
            k = along(u, 0, s)
            remote(
                grad.at[block_rows([k]), cols], s1.at[u, s - 1],
                rs0_sem.at[NU], rs0_sem.at[u], peer_of(u, 0, s),
            ).start()

    def rs0_receive(u):
        arrived(s1.at[u], rs0_sem.at[u])
        own = grad[block_rows([along(u, 0, 0)]), cols_of(u)]
        r1[u] = own + s1[u, 0] + s1[u, 1] + s1[u, 2]
        for s in OFFSETS:
            k = along(u, 1, s)
            remote(
                r1.at[u, ds(k * 32, 32, 32)], s2.at[u, s - 1],
                rs1_sem.at[NU], rs1_sem.at[u], peer_of(u, 1, s),
            ).start()

    def rs1_receive(u):
        arrived(s2.at[u], rs1_sem.at[u])
        own = r1[u, ds(along(u, 1, 0) * 32, 32, 32)]
        k = along(u, 2, 0)
        s3[u, k] = own + s2[u, 0] + s2[u, 1] + s2[u, 2]
        for s in OFFSETS:
            remote(
                s3.at[u, k], s3.at[u, k], x_sem.at[NU], x_sem.at[u], peer_of(u, 2, s)
            ).start()

    rescale = 1.0 / math.sqrt(TOTAL_MEM * TOTAL_CELLS)

    def x_receive(u):
        arrived(s3.at[u, pl.ds(0, 3)], x_sem.at[u])
        at = (block_rows([along(u, 0, 0), along(u, 1, 0)]), cols_of(u))
        full[at] = (s3[u, 0] + s3[u, 1] + s3[u, 2] + s3[u, 3]) * rescale
        for s in OFFSETS:
            remote(
                full.at[at], full.at[at], ag1_sem.at[NU], ag1_sem.at[u], peer_of(u, 1, s)
            ).start()

    def to_core(u, s):
        at = (block_rows([along(u, 0, s)]), cols_of(u))
        remote(full.at[at], full.at[at], cg_sem.at[NU], cg_sem.at[u], other_core).start()

    def ag1_receive(u):
        arrived(full.at[pl.ds(0, 96), cols_of(u)], ag1_sem.at[u])
        at = (block_rows([along(u, 0, 0)]), cols_of(u))
        for s in OFFSETS:
            remote(
                full.at[at], full.at[at], ag0_sem.at[NU], ag0_sem.at[u], peer_of(u, 0, s)
            ).start()
        to_core(u, 0)

    def ag0_receive(u):
        arrived(full.at[pl.ds(0, 384), cols_of(u)], ag0_sem.at[u])
        for s in OFFSETS:
            to_core(u, s)

    def cg_receive(u):
        arrived(full.at[pl.ds(0, HALF), cols_of(u)], cg_sem.at[u])

    def run():
        load()
        greet()
        small_operands()
        w1_copy.wait()
        w1t[...] = w1[...].T
        forward(0)
        pl.semaphore_wait(barrier, 23)
        send_all(0, fs, fr, f_sem)
        send_area()
        forward(1)
        send_all(1, fs, fr, f_sem)
        forward(2)
        send_all(2, fs, fr, f_sem)
        arrived(av.at[pl.ds(0, 15)], area_sem.at[1])
        receive_all(0, fr, f_sem)
        pairwise(0)
        send_all(0, gs, gr, g_sem)
        forward(3)
        send_all(3, fs, fr, f_sem)
        receive_all(1, fr, f_sem)
        pairwise(1)
        send_all(1, gs, gr, g_sem)
        receive_all(2, fr, f_sem)
        pairwise(2)
        send_all(2, gs, gr, g_sem)
        receive_all(0, gr, g_sem)
        backward(0)
        receive_all(3, fr, f_sem)
        pairwise(3)
        send_all(3, gs, gr, g_sem)
        receive_all(1, gr, g_sem)
        backward(1)
        weight_gradients(0, 2, 0)
        weight_gradients(0, 2, 1)
        receive_all(2, gr, g_sem)
        backward(2)
        receive_all(3, gr, g_sem)
        backward(3)
        own_loss = jnp.sum(loss[...], keepdims=True)
        row = lax.broadcasted_iota(jnp.int32, (8, VP), 0)
        col = lax.broadcasted_iota(jnp.int32, (8, VP), 1)
        grad[0:8, H:WIDE] += jnp.where((row == 0) & (col == LOSS_COL), own_loss, 0.0)
        last = pl.ds(2 * CQ, 2 * CQ)
        for j in range(4):
            grad_in_tile(last, 1 - core, j, False)
            core_send(2 * j)
            core_send(2 * j + 1)
        grad_out_tile(last, 1 - core, False)
        core_send(NU - 1)
        grad_in_tile(last, core, 0, False)
        core_receive(0)
        grad_in_tile(last, core, 1, False)
        core_receive(1)
        grad_in_tile(last, core, 2, False)
        core_receive(2)
        core_receive(3)
        grad_in_tile(last, core, 3, False)
        core_receive(4)
        grad_out_tile(last, core, False)
        core_receive(5)
        embedding_derivative(0, 0)
        core_receive(6)
        core_receive(7)
        core_receive(8)
        waves = ((0, 1, 2), (3, 4, 5), (6, 7, 8))

        def each(step, wave):
            for u in waves[wave]:
                step(u)

        embedding_derivative(1, 0)
        each(rs0_receive, 0)
        embedding_derivative(0, 1)
        each(rs0_receive, 1)
        each(rs1_receive, 0)
        embedding_derivative(1, 1)
        each(rs0_receive, 2)
        each(rs1_receive, 1)
        each(x_receive, 0)
        each(rs1_receive, 2)
        each(x_receive, 1)
        each(ag1_receive, 0)
        each(x_receive, 2)
        each(ag1_receive, 1)
        each(ag1_receive, 2)
        each(ag0_receive, 0)
        each(ag0_receive, 1)
        each(ag0_receive, 2)
        for wave in range(3):
            each(cg_receive, wave)

    run()
    left(av.at[pl.ds(0, 15)], area_sem.at[0])
    left(fs.at[:, pl.ds(0, 7)], f_sem.at[NQ])
    left(gs.at[:, pl.ds(0, 7)], g_sem.at[NQ])
    left(core_in, core_sem.at[NU])
    left(s1, rs0_sem.at[NU])
    left(s2, rs1_sem.at[NU])
    left(s3.at[:, pl.ds(0, 3)], x_sem.at[NU])
    left(s2, ag1_sem.at[NU])
    left(s1, ag0_sem.at[NU])
    left(core_in, cg_sem.at[NU])


def finish(ed, full, ed_out, grad_out, grad_t_out, penalty, sem):
    ed_copy = pltpu.make_async_copy(ed, ed_out, sem.at[0])
    ed_copy.start()
    grad_copy = pltpu.make_async_copy(full.at[:, 0:H], grad_out, sem.at[1])
    grad_copy.start()
    t = full[:, H:WIDE].T
    grad_t_out[...] = jnp.concatenate([t[VG * r : VG * r + VH] for r in range(NR)], axis=0)
    rescale = 1.0 / math.sqrt(TOTAL_MEM * TOTAL_CELLS)
    at = full[0:1, H + LOSS_COL : H + LOSS_COL + 1]
    penalty[...] = at * (1.0 / (rescale * TOTAL_CELLS * V))
    ed_copy.wait()
    grad_copy.wait()


def per_device(
    embedding_tensor,
    first_projection_matrix,
    variable_projection_matrix,
    target,
    var_weight,
    area_weight,
):
    vmem = pl.BlockSpec(memory_space=pltpu.VMEM)
    hbm = pl.BlockSpec(memory_space=pl.ANY)
    dma = pltpu.SemaphoreType.DMA
    big = (MEM, H, CELLS)
    swap = (NQ, 8, MEM, VH, 128)
    in_vmem = (pltpu.VMEM(big, BF16), pltpu.VMEM((H, WIDE), F32))
    ed, full = pl.pallas_call(
        kernel,
        name="decoder_crps",
        out_shape=in_vmem,
        in_specs=[hbm] * 6,
        out_specs=(vmem, vmem),
        scratch_shapes=[
            pltpu.VMEM(big, BF16),
            pltpu.VMEM((H, H), BF16),
            pltpu.VMEM((H, H), BF16),
            pltpu.VMEM((V, H), BF16),
            pltpu.VMEM((V, CELLS), BF16),
            pltpu.VMEM((1, V), F32),
            pltpu.VMEM((8, 128), F32),
            pltpu.VMEM((H, VP), BF16),
            pltpu.VMEM((VP, H), BF16),
            pltpu.VMEM(big, BF16),
            pltpu.VMEM(big, F32),
            pltpu.VMEM((MEM, VP, CELLS), BF16),
            pltpu.VMEM(big, BF16),
            pltpu.VMEM((NR, VH, CELLS), F32),
            pltpu.VMEM((NR, VH, 128), F32),
            pltpu.VMEM((16, 8, 128), F32),
            pltpu.VMEM(swap, F32),
            pltpu.VMEM(swap, F32),
            pltpu.VMEM(swap, F32),
            pltpu.VMEM(swap, F32),
            pltpu.VMEM((H, WIDE), F32),
            pltpu.VMEM((HALF, WIDE), F32),
            pltpu.VMEM((NU, 3, 128, 128), F32),
            pltpu.VMEM((NU, 128, 128), F32),
            pltpu.VMEM((NU, 3, 32, 128), F32),
            pltpu.VMEM((NU, 4, 32, 128), F32),
            pltpu.VMEM((8, 128), F32),
            dma((NQ + 5,)),
            dma((2,)),
            dma((NQ + 1,)), dma((NQ + 1,)),
            dma((NU + 1,)), dma((NU + 1,)), dma((NU + 1,)), dma((NU + 1,)),
            dma((NU + 1,)), dma((NU + 1,)), dma((NU + 1,)),
        ],
        compiler_params=pltpu.CompilerParams(
            collective_id=0, has_side_effects=True, vmem_limit_bytes=50 * 2**20
        ),
        cost_estimate=pl.CostEstimate(
            flops=15_000_000_000, bytes_accessed=20_000_000, transcendentals=4_000_000
        ),
    )(
        embedding_tensor,
        first_projection_matrix,
        variable_projection_matrix.T,
        target,
        var_weight.reshape(1, V),
        area_weight.reshape(8, 128),
    )
    ed, grad_in, grad_out_t, penalty = pl.pallas_call(
        finish,
        name="write_out",
        out_shape=(
            jax.ShapeDtypeStruct(big, BF16),
            jax.ShapeDtypeStruct((H, H), F32),
            jax.ShapeDtypeStruct((V, H), F32),
            jax.ShapeDtypeStruct((1, 1), F32),
        ),
        in_specs=[vmem, vmem],
        out_specs=(hbm, hbm, vmem, vmem),
        scratch_shapes=[dma((2,))],
        compiler_params=pltpu.CompilerParams(vmem_limit_bytes=8 * 2**20),
    )(ed, full)
    return ed, grad_in, grad_out_t.T, penalty[0, 0]


def solution(mesh):
    in_specs = (P("member", None, "grid"), P(), P(), P(None, "grid"), P(), P("grid"))
    out_specs = (P("member", None, "grid"), P(), P(), P())
    return jax.shard_map(
        per_device, mesh=mesh, in_specs=in_specs, out_specs=out_specs, check_vma=False
    )
```

```python
import functools
import math

import jax
import jax.numpy as jnp
from jax import lax
from jax.experimental import pallas as pl
from jax.experimental.pallas import tpu as pltpu
from jax.sharding import PartitionSpec as P

SMOOTH_WIDTH = 0.1
ALPHA_FAIR = 0.95
MESH = pl.DeviceIdType.MESH
F32 = jnp.float32
BF16 = jnp.bfloat16
GELU_A = math.sqrt(2.0 / math.pi)
GELU_B = 0.044715

H = 1024
V = 100
CELLS = 1024
MEM = 2
TOTAL_MEM = 16
TOTAL_CELLS = 16384
NQ = 4
CQ = CELLS // NQ
NL = CQ // 128
NR = 8 // NL
VH = V // NR
VG = 128 // NR
VP = NR * VG
HALF = H // 2
WIDE = H + VP
NU = WIDE // 128
LOSS_COL = VH
ORDERS = (("x", "y", "z"), ("y", "z", "x"), ("z", "x", "y"))
OFFSETS = (2, 1, 3)


def dot(a, b):
    return lax.dot_general(a, b, (((1,), (0,)), ((), ())), preferred_element_type=F32)


def dot_t(a, b):
    return lax.dot_general(a, b, (((1,), (1,)), ((), ())), preferred_element_type=F32)


def gelu_and_derivative(x):
    x2 = x * x
    t = jnp.tanh(x * (GELU_A + (GELU_A * GELU_B) * x2))
    h = 0.5 + 0.5 * t
    y = x * h
    return y, h + (y * (1.0 - t)) * (GELU_A + (3.0 * GELU_A * GELU_B) * x2)


def ds(start, size, multiple):
    return pl.ds(pl.multiple_of(start, multiple), size)


def kernel(
    emb, w1_hbm, w2_hbm, target_hbm, vw_hbm, aw_hbm,
    ed, full,
    e, w1, w1t, w2_in, target, vw, aw, w2p, w2t, act, dg, gv, gp, tgt, vcol, av,
    fs, fr, gs, gr, grad, core_in, s1, r1, s2, s3, loss,
    in_sem, area_sem, f_sem, g_sem, core_sem, rs0_sem, rs1_sem, x_sem, ag1_sem, ag0_sem, cg_sem,
):
    me = lax.axis_index("member")
    g = lax.axis_index("grid")
    pos = {"x": me % 4, "y": (g // 8) * 2 + me // 4, "z": (g // 2) % 4, "c": g % 2}
    core = pos["c"]

    def device(p):
        return ((p["y"] % 2) * 4 + p["x"], ((p["y"] // 2) * 4 + p["z"]) * 2 + p["c"])

    def moved(**by):
        return {k: (v + by[k]) % (2 if k == "c" else 4) if k in by else v for k, v in pos.items()}

    def remote(src, dst, send_sem, recv_sem, to):
        return pltpu.make_async_remote_copy(
            src_ref=src, dst_ref=dst, send_sem=send_sem, recv_sem=recv_sem,
            device_id=to, device_id_type=MESH,
        )

    other_core = device(moved(c=1))

    def arrived(ref, sem):
        remote(ref, ref, sem, sem, other_core).wait_recv()

    def left(ref, sem):
        remote(ref, ref, sem, sem, other_core).wait_send()

    def member_peer(o):
        return (me // 4 + o // 4) % 2 * 4 + (me % 4 + o % 4) % 4

    def emb_copy(q):
        sl = pl.ds(q * CQ, CQ)
        return pltpu.make_async_copy(emb.at[:, :, sl], e.at[:, :, sl], in_sem.at[q])

    w1_copy = pltpu.make_async_copy(w1_hbm, w1, in_sem.at[NQ])
    small_copies = [
        pltpu.make_async_copy(src, dst, in_sem.at[NQ + 1 + i])
        for i, (src, dst) in enumerate(
            ((w2_hbm, w2_in), (target_hbm, target), (vw_hbm, vw), (aw_hbm, aw))
        )
    ]
    barrier = pltpu.get_barrier_semaphore()

    def load():
        w1_copy.start()
        for copy in small_copies:
            copy.start()
        for q in range(NQ):
            emb_copy(q).start()

    def greet():
        peers = [(member_peer(o), g) for o in range(1, 8)]
        peers += [(me, (g + o) % 16) for o in range(1, 16)]
        peers += [((me + 4) % 8, (g + 8) % 16)]
        for peer in peers:
            pl.semaphore_signal(barrier, inc=1, device_id=peer, device_id_type=MESH)

    def small_operands():
        for copy in small_copies:
            copy.wait()
        wide = w2_in[...].astype(F32)
        gap = jnp.zeros((VG - VH, H), F32)
        groups = []
        for r in range(NR):
            groups += [wide[r * VH : r * VH + VH], gap]
        w2t[...] = jnp.concatenate(groups, axis=0).astype(BF16)
        w2p[...] = w2t[...].T
        t32 = target[...].astype(F32)
        columns = jnp.broadcast_to(vw[...], (128, V)).T
        for r in range(NR):
            tgt[r] = t32[r * VH : r * VH + VH]
            vcol[r] = columns[r * VH : r * VH + VH]
        av[g] = aw[...]
        loss[...] = jnp.zeros_like(loss)

    def send_area():
        for o in range(1, 16):
            remote(
                av.at[g], av.at[g], area_sem.at[0], area_sem.at[1], (me, (g + o) % 16)
            ).start()

    PEERS = (6, 2, 5, 7, 4, 1, 3)

    def send_all(q, src, dst, sem):
        for o in PEERS:
            peer = member_peer(o)
            remote(src.at[q, peer], dst.at[q, me], sem.at[NQ], sem.at[q], (peer, g)).start()
        dst[q, me] = src[q, me]

    def receive_all(q, dst, sem):
        arrived(dst.at[q, pl.ds(0, 7)], sem.at[q])

    def forward(q):
        sl = pl.ds(q * CQ, CQ)
        emb_copy(q).wait()

        for m in range(MEM):
            y, d = gelu_and_derivative(dot(w1t[...], e[m, :, sl]))
            act[m, :, sl] = y.astype(BF16)
            dg[m, :, sl] = d
            fc = dot(w2t[...], act[m, :, sl])
            for r in range(NR):
                for l in range(NL):
                    fs[q, r * NL + l, m] = fc[VG * r : VG * r + VH, 128 * l : 128 * l + 128]

    coef = (1.0 - (1.0 - ALPHA_FAIR) / TOTAL_MEM) / (TOTAL_MEM - 1)
    d2 = SMOOTH_WIDTH * SMOOTH_WIDTH

    def pairwise(q):
        mine_r, mine_l = me // NL, me % NL
        lanes = ds(q * CQ + mine_l * 128, 128, 128)
        mean = jnp.sum(jnp.sum(av[...], axis=0), keepdims=True) / TOTAL_CELLS
        area = aw[pl.ds(q * NL + mine_l, 1), :] / mean

        def tile(rows, n):
            scale = area * vcol[mine_r, rows, :]
            t = tgt[mine_r, rows, lanes]
            f = [fr[q, k // 2, k % 2, rows, :] for k in range(TOTAL_MEM)]
            s = [None] * TOTAL_MEM
            spread = None
            for i in range(TOTAL_MEM):
                for k in range(i + 1, TOTAL_MEM):
                    d = f[i] - f[k]
                    w = d * d + d2
                    inv = lax.rsqrt(w)
                    slope = d * inv
                    s[i] = slope if s[i] is None else s[i] + slope
                    s[k] = -slope if s[k] is None else s[k] - slope
                    smooth = w * inv - SMOOTH_WIDTH
                    spread = smooth if spread is None else spread + smooth
            truth = None
            for i in range(TOTAL_MEM):
                d = f[i] - t
                w = d * d + d2
                inv = lax.rsqrt(w)
                gs[q, i // 2, i % 2, rows, :] = scale * (d * inv - coef * s[i])
                smooth = w * inv - SMOOTH_WIDTH
                truth = smooth if truth is None else truth + smooth
            loss[0:n, :] += scale * (truth / TOTAL_MEM - (coef / TOTAL_MEM) * spread)

        for i in range(0, VH, 8):
            tile(pl.ds(i, min(8, VH - i)), min(8, VH - i))

    def backward(q):
        sl = pl.ds(q * CQ, CQ)
        gap = jnp.zeros((VG - VH, 128), F32)

        for m in range(MEM):
            for l in range(NL):
                groups = []
                for r in range(NR):
                    groups += [gr[q, r * NL + l, m], gap]
                at = q * CQ + 128 * l
                gv[m, :, at : at + 128] = jnp.concatenate(groups, axis=0).astype(BF16)
            gp[m, :, sl] = (dot(w2p[...], gv[m, :, sl]) * dg[m, :, sl]).astype(BF16)

    def add_to_grad(rows, cols, new, first):
        if first:
            grad[rows, cols] = new
        else:
            grad[rows, cols] += new

    def grad_in_tile(sl, half, j, first):
        rows, cols = ds(half * HALF, HALF, HALF), ds(j * 256, 256, 256)
        new = dot_t(e[0, rows, sl], gp[0, cols, sl]) + dot_t(e[1, rows, sl], gp[1, cols, sl])
        add_to_grad(rows, cols, new, first)

    def grad_out_tile(sl, half, first):
        rows = ds(half * HALF, HALF, HALF)
        new = dot_t(act[0, rows, sl], gv[0, :, sl]) + dot_t(act[1, rows, sl], gv[1, :, sl])
        add_to_grad(rows, pl.ds(H, VP), new, first)

    def weight_gradients(q, n, half):
        sl = pl.ds(q * CQ, n * CQ)

        for j in range(4):
            grad_in_tile(sl, half, j, q == 0)

        grad_out_tile(sl, half, q == 0)

    def embedding_derivative(m, q):
        sl = pl.ds(q * 512, 512)
        ed[m, :, sl] = dot(w1[...], gp[m, :, sl]).astype(BF16)

    def cols_of(u):
        return pl.ds(u * 128, 128)

    def along(u, level, s):
        return (pos[ORDERS[u % 3][level]] + s) % 4

    def peer_of(u, level, s):
        return device(moved(**{ORDERS[u % 3][level]: s}))

    def block_rows(ks):
        begin = core * HALF
        for k, size in zip(ks, (128, 32)):
            begin = begin + k * size
        size = (128, 32)[len(ks) - 1]
        return ds(begin, size, size)

    def core_send(u):
        remote(
            grad.at[ds((1 - core) * HALF, HALF, HALF), cols_of(u)], core_in.at[:, cols_of(u)],
            core_sem.at[NU], core_sem.at[u], other_core,
        ).start()

    def core_receive(u):
        cols = cols_of(u)
        arrived(core_in.at[:, cols], core_sem.at[u])
        grad[ds(core * HALF, HALF, HALF), cols] += core_in[:, cols]
        for s in OFFSETS:
            k = along(u, 0, s)
            remote(
                grad.at[block_rows([k]), cols], s1.at[u, s - 1],
                rs0_sem.at[NU], rs0_sem.at[u], peer_of(u, 0, s),
            ).start()

    def rs0_receive(u):
        arrived(s1.at[u], rs0_sem.at[u])
        own = grad[block_rows([along(u, 0, 0)]), cols_of(u)]
        r1[u] = own + s1[u, 0] + s1[u, 1] + s1[u, 2]
        for s in OFFSETS:
            k = along(u, 1, s)
            remote(
                r1.at[u, ds(k * 32, 32, 32)], s2.at[u, s - 1],
                rs1_sem.at[NU], rs1_sem.at[u], peer_of(u, 1, s),
            ).start()

    def rs1_receive(u):
        arrived(s2.at[u], rs1_sem.at[u])
        own = r1[u, ds(along(u, 1, 0) * 32, 32, 32)]
        k = along(u, 2, 0)
        s3[u, k] = own + s2[u, 0] + s2[u, 1] + s2[u, 2]
        for s in OFFSETS:
            remote(
                s3.at[u, k], s3.at[u, k], x_sem.at[NU], x_sem.at[u], peer_of(u, 2, s)
            ).start()

    rescale = 1.0 / math.sqrt(TOTAL_MEM * TOTAL_CELLS)

    def x_receive(u):
        arrived(s3.at[u, pl.ds(0, 3)], x_sem.at[u])
        at = (block_rows([along(u, 0, 0), along(u, 1, 0)]), cols_of(u))
        full[at] = (s3[u, 0] + s3[u, 1] + s3[u, 2] + s3[u, 3]) * rescale
        for s in OFFSETS:
            remote(
                full.at[at], full.at[at], ag1_sem.at[NU], ag1_sem.at[u], peer_of(u, 1, s)
            ).start()

    def to_core(u, s):
        at = (block_rows([along(u, 0, s)]), cols_of(u))
        remote(full.at[at], full.at[at], cg_sem.at[NU], cg_sem.at[u], other_core).start()

    def ag1_receive(u):
        arrived(full.at[pl.ds(0, 96), cols_of(u)], ag1_sem.at[u])
        at = (block_rows([along(u, 0, 0)]), cols_of(u))
        for s in OFFSETS:
            remote(
                full.at[at], full.at[at], ag0_sem.at[NU], ag0_sem.at[u], peer_of(u, 0, s)
            ).start()
        to_core(u, 0)

    def ag0_receive(u):
        arrived(full.at[pl.ds(0, 384), cols_of(u)], ag0_sem.at[u])
        for s in OFFSETS:
            to_core(u, s)

    def cg_receive(u):
        arrived(full.at[pl.ds(0, HALF), cols_of(u)], cg_sem.at[u])

    def run():
        load()
        greet()
        small_operands()
        w1_copy.wait()
        w1t[...] = w1[...].T
        forward(0)
        pl.semaphore_wait(barrier, 23)
        send_all(0, fs, fr, f_sem)
        send_area()
        forward(1)
        send_all(1, fs, fr, f_sem)
        forward(2)
        send_all(2, fs, fr, f_sem)
        arrived(av.at[pl.ds(0, 15)], area_sem.at[1])
        receive_all(0, fr, f_sem)
        pairwise(0)
        send_all(0, gs, gr, g_sem)
        forward(3)
        send_all(3, fs, fr, f_sem)
        receive_all(1, fr, f_sem)
        pairwise(1)
        send_all(1, gs, gr, g_sem)
        receive_all(2, fr, f_sem)
        pairwise(2)
        send_all(2, gs, gr, g_sem)
        receive_all(0, gr, g_sem)
        backward(0)
        receive_all(3, fr, f_sem)
        pairwise(3)
        send_all(3, gs, gr, g_sem)
        receive_all(1, gr, g_sem)
        backward(1)
        weight_gradients(0, 2, 0)
        weight_gradients(0, 2, 1)
        receive_all(2, gr, g_sem)
        backward(2)
        receive_all(3, gr, g_sem)
        backward(3)
        own_loss = jnp.sum(loss[...], keepdims=True)
        row = lax.broadcasted_iota(jnp.int32, (8, VP), 0)
        col = lax.broadcasted_iota(jnp.int32, (8, VP), 1)
        grad[0:8, H:WIDE] += jnp.where((row == 0) & (col == LOSS_COL), own_loss, 0.0)
        last = pl.ds(2 * CQ, 2 * CQ)
        for j in range(4):
            grad_in_tile(last, 1 - core, j, False)
            core_send(2 * j)
            core_send(2 * j + 1)
        grad_out_tile(last, 1 - core, False)
        core_send(NU - 1)
        grad_in_tile(last, core, 0, False)
        core_receive(0)
        grad_in_tile(last, core, 1, False)
        core_receive(1)
        grad_in_tile(last, core, 2, False)
        core_receive(2)
        core_receive(3)
        grad_in_tile(last, core, 3, False)
        core_receive(4)
        grad_out_tile(last, core, False)
        core_receive(5)
        waves = ((0, 1, 2), (3, 4, 5), (6, 7, 8))

        def each(step, wave):
            for u in waves[wave]:
                step(u)

        embedding_derivative(0, 0)
        each(rs0_receive, 0)
        each(core_receive, 2)
        embedding_derivative(1, 0)
        each(rs0_receive, 1)
        each(rs1_receive, 0)
        embedding_derivative(0, 1)
        each(rs0_receive, 2)
        each(rs1_receive, 1)
        each(x_receive, 0)
        each(rs1_receive, 2)
        each(x_receive, 1)
        each(ag1_receive, 0)
        each(x_receive, 2)
        embedding_derivative(1, 1)
        each(ag1_receive, 1)
        each(ag1_receive, 2)
        each(ag0_receive, 0)
        each(ag0_receive, 1)
        each(ag0_receive, 2)
        for wave in range(3):
            each(cg_receive, wave)

    run()
    left(av.at[pl.ds(0, 15)], area_sem.at[0])
    left(fs.at[:, pl.ds(0, 7)], f_sem.at[NQ])
    left(gs.at[:, pl.ds(0, 7)], g_sem.at[NQ])
    left(core_in, core_sem.at[NU])
    left(s1, rs0_sem.at[NU])
    left(s2, rs1_sem.at[NU])
    left(s3.at[:, pl.ds(0, 3)], x_sem.at[NU])
    left(s2, ag1_sem.at[NU])
    left(s1, ag0_sem.at[NU])
    left(core_in, cg_sem.at[NU])


def finish(ed, full, ed_out, grad_out, grad_t_out, penalty, sem):
    ed_copy = pltpu.make_async_copy(ed, ed_out, sem.at[0])
    ed_copy.start()
    grad_copy = pltpu.make_async_copy(full.at[:, 0:H], grad_out, sem.at[1])
    grad_copy.start()
    t = full[:, H:WIDE].T
    grad_t_out[...] = jnp.concatenate([t[VG * r : VG * r + VH] for r in range(NR)], axis=0)
    rescale = 1.0 / math.sqrt(TOTAL_MEM * TOTAL_CELLS)
    at = full[0:1, H + LOSS_COL : H + LOSS_COL + 1]
    penalty[...] = at * (1.0 / (rescale * TOTAL_CELLS * V))
    ed_copy.wait()
    grad_copy.wait()


def per_device(
    embedding_tensor,
    first_projection_matrix,
    variable_projection_matrix,
    target,
    var_weight,
    area_weight,
):
    vmem = pl.BlockSpec(memory_space=pltpu.VMEM)
    hbm = pl.BlockSpec(memory_space=pl.ANY)
    dma = pltpu.SemaphoreType.DMA
    big = (MEM, H, CELLS)
    swap = (NQ, 8, MEM, VH, 128)
    in_vmem = (pltpu.VMEM(big, BF16), pltpu.VMEM((H, WIDE), F32))
    ed, full = pl.pallas_call(
        kernel,
        name="decoder_crps",
        out_shape=in_vmem,
        in_specs=[hbm] * 6,
        out_specs=(vmem, vmem),
        scratch_shapes=[
            pltpu.VMEM(big, BF16),
            pltpu.VMEM((H, H), BF16),
            pltpu.VMEM((H, H), BF16),
            pltpu.VMEM((V, H), BF16),
            pltpu.VMEM((V, CELLS), BF16),
            pltpu.VMEM((1, V), F32),
            pltpu.VMEM((8, 128), F32),
            pltpu.VMEM((H, VP), BF16),
            pltpu.VMEM((VP, H), BF16),
            pltpu.VMEM(big, BF16),
            pltpu.VMEM(big, F32),
            pltpu.VMEM((MEM, VP, CELLS), BF16),
            pltpu.VMEM(big, BF16),
            pltpu.VMEM((NR, VH, CELLS), F32),
            pltpu.VMEM((NR, VH, 128), F32),
            pltpu.VMEM((16, 8, 128), F32),
            pltpu.VMEM(swap, F32),
            pltpu.VMEM(swap, F32),
            pltpu.VMEM(swap, F32),
            pltpu.VMEM(swap, F32),
            pltpu.VMEM((H, WIDE), F32),
            pltpu.VMEM((HALF, WIDE), F32),
            pltpu.VMEM((NU, 3, 128, 128), F32),
            pltpu.VMEM((NU, 128, 128), F32),
            pltpu.VMEM((NU, 3, 32, 128), F32),
            pltpu.VMEM((NU, 4, 32, 128), F32),
            pltpu.VMEM((8, 128), F32),
            dma((NQ + 5,)),
            dma((2,)),
            dma((NQ + 1,)), dma((NQ + 1,)),
            dma((NU + 1,)), dma((NU + 1,)), dma((NU + 1,)), dma((NU + 1,)),
            dma((NU + 1,)), dma((NU + 1,)), dma((NU + 1,)),
        ],
        compiler_params=pltpu.CompilerParams(
            collective_id=0, has_side_effects=True, vmem_limit_bytes=50 * 2**20
        ),
        cost_estimate=pl.CostEstimate(
            flops=15_000_000_000, bytes_accessed=20_000_000, transcendentals=4_000_000
        ),
    )(
        embedding_tensor,
        first_projection_matrix,
        variable_projection_matrix.T,
        target,
        var_weight.reshape(1, V),
        area_weight.reshape(8, 128),
    )
    ed, grad_in, grad_out_t, penalty = pl.pallas_call(
        finish,
        name="write_out",
        out_shape=(
            jax.ShapeDtypeStruct(big, BF16),
            jax.ShapeDtypeStruct((H, H), F32),
            jax.ShapeDtypeStruct((V, H), F32),
            jax.ShapeDtypeStruct((1, 1), F32),
        ),
        in_specs=[vmem, vmem],
        out_specs=(hbm, hbm, vmem, vmem),
        scratch_shapes=[dma((2,))],
        compiler_params=pltpu.CompilerParams(vmem_limit_bytes=8 * 2**20),
    )(ed, full)
    return ed, grad_in, grad_out_t.T, penalty[0, 0]


def solution(mesh):
    in_specs = (P("member", None, "grid"), P(), P(), P(None, "grid"), P(), P("grid"))
    out_specs = (P("member", None, "grid"), P(), P(), P())
    return jax.shard_map(
        per_device, mesh=mesh, in_specs=in_specs, out_specs=out_specs, check_vma=False
    )
```

```python
import functools
import math

import jax
import jax.numpy as jnp
from jax import lax
from jax.experimental import pallas as pl
from jax.experimental.pallas import tpu as pltpu
from jax.sharding import PartitionSpec as P

SMOOTH_WIDTH = 0.1
ALPHA_FAIR = 0.95
MESH = pl.DeviceIdType.MESH
F32 = jnp.float32
BF16 = jnp.bfloat16
GELU_A = math.sqrt(2.0 / math.pi)
GELU_B = 0.044715

H = 1024
V = 100
CELLS = 1024
MEM = 2
TOTAL_MEM = 16
TOTAL_CELLS = 16384
NQ = 4
CQ = CELLS // NQ
NL = CQ // 128
NR = 8 // NL
VH = V // NR
VG = 128 // NR
VP = NR * VG
HALF = H // 2
WIDE = H + VP
NU = WIDE // 128
LOSS_COL = VH
ORDERS = (("x", "y", "z"), ("y", "z", "x"), ("z", "x", "y"))
OFFSETS = (2, 1, 3)


def dot(a, b):
    return lax.dot_general(a, b, (((1,), (0,)), ((), ())), preferred_element_type=F32)


def dot_t(a, b):
    return lax.dot_general(a, b, (((1,), (1,)), ((), ())), preferred_element_type=F32)


def gelu_and_derivative(x):
    x2 = x * x
    t = jnp.tanh(x * (GELU_A + (GELU_A * GELU_B) * x2))
    h = 0.5 + 0.5 * t
    y = x * h
    return y, h + (y * (1.0 - t)) * (GELU_A + (3.0 * GELU_A * GELU_B) * x2)


def ds(start, size, multiple):
    return pl.ds(pl.multiple_of(start, multiple), size)


def kernel(
    emb, w1_hbm, w2_hbm, target_hbm, vw_hbm, aw_hbm,
    ed, full,
    e, w1, w1t, w2_in, target, vw, aw, w2p, w2t, act, dg, gv, gp, tgt, vcol, av,
    fs, fr, gs, gr, grad, core_in, s1, r1, s2, s3, loss,
    in_sem, area_sem, f_sem, g_sem, core_sem, rs0_sem, rs1_sem, x_sem, ag1_sem, ag0_sem, cg_sem,
):
    me = lax.axis_index("member")
    g = lax.axis_index("grid")
    pos = {"x": me % 4, "y": (g // 8) * 2 + me // 4, "z": (g // 2) % 4, "c": g % 2}
    core = pos["c"]

    def device(p):
        return ((p["y"] % 2) * 4 + p["x"], ((p["y"] // 2) * 4 + p["z"]) * 2 + p["c"])

    def moved(**by):
        return {k: (v + by[k]) % (2 if k == "c" else 4) if k in by else v for k, v in pos.items()}

    def remote(src, dst, send_sem, recv_sem, to):
        return pltpu.make_async_remote_copy(
            src_ref=src, dst_ref=dst, send_sem=send_sem, recv_sem=recv_sem,
            device_id=to, device_id_type=MESH,
        )

    other_core = device(moved(c=1))

    def arrived(ref, sem):
        remote(ref, ref, sem, sem, other_core).wait_recv()

    def left(ref, sem):
        remote(ref, ref, sem, sem, other_core).wait_send()

    def member_peer(o):
        return (me // 4 + o // 4) % 2 * 4 + (me % 4 + o % 4) % 4

    def emb_copy(q):
        sl = pl.ds(q * CQ, CQ)
        return pltpu.make_async_copy(emb.at[:, :, sl], e.at[:, :, sl], in_sem.at[q])

    w1_copy = pltpu.make_async_copy(w1_hbm, w1, in_sem.at[NQ])
    small_copies = [
        pltpu.make_async_copy(src, dst, in_sem.at[NQ + 1 + i])
        for i, (src, dst) in enumerate(
            ((w2_hbm, w2_in), (target_hbm, target), (vw_hbm, vw), (aw_hbm, aw))
        )
    ]
    barrier = pltpu.get_barrier_semaphore()

    def load():
        for copy in small_copies:
            copy.start()
        w1_copy.start()
        for q in range(NQ):
            emb_copy(q).start()

    def greet():
        peers = [(member_peer(o), g) for o in range(1, 8)]
        peers += [(me, (g + o) % 16) for o in range(1, 16)]
        peers += [((me + 4) % 8, (g + 8) % 16)]
        for peer in peers:
            pl.semaphore_signal(barrier, inc=1, device_id=peer, device_id_type=MESH)

    def small_operands():
        for copy in small_copies:
            copy.wait()
        wide = w2_in[...].astype(F32)
        gap = jnp.zeros((VG - VH, H), F32)
        groups = []
        for r in range(NR):
            groups += [wide[r * VH : r * VH + VH], gap]
        w2t[...] = jnp.concatenate(groups, axis=0).astype(BF16)
        w2p[...] = w2t[...].T
        t32 = target[...].astype(F32)
        columns = jnp.broadcast_to(vw[...], (128, V)).T
        for r in range(NR):
            tgt[r] = t32[r * VH : r * VH + VH]
            vcol[r] = columns[r * VH : r * VH + VH]
        av[g] = aw[...]
        loss[...] = jnp.zeros_like(loss)

    def send_area():
        for o in range(1, 16):
            remote(
                av.at[g], av.at[g], area_sem.at[0], area_sem.at[1], (me, (g + o) % 16)
            ).start()

    PEERS = (6, 2, 5, 7, 4, 1, 3)

    def send_all(q, src, dst, sem):
        for o in PEERS:
            peer = member_peer(o)
            remote(src.at[q, peer], dst.at[q, me], sem.at[NQ], sem.at[q], (peer, g)).start()
        dst[q, me] = src[q, me]

    def receive_all(q, dst, sem):
        arrived(dst.at[q, pl.ds(0, 7)], sem.at[q])

    def send_member(q, m):
        for o in PEERS:
            peer = member_peer(o)
            remote(
                fs.at[q, peer, m], fr.at[q, me, m], f_sem.at[NQ], f_sem.at[q], (peer, g)
            ).start()
        fr[q, me, m] = fs[q, me, m]

    def forward(q, members=range(MEM)):
        sl = pl.ds(q * CQ, CQ)
        if 0 in members:
            emb_copy(q).wait()
        for m in members:
            y, d = gelu_and_derivative(dot(w1t[...], e[m, :, sl]))
            act[m, :, sl] = y.astype(BF16)
            dg[m, :, sl] = d
            fc = dot(w2t[...], act[m, :, sl])
            for r in range(NR):
                for l in range(NL):
                    fs[q, r * NL + l, m] = fc[VG * r : VG * r + VH, 128 * l : 128 * l + 128]

    coef = (1.0 - (1.0 - ALPHA_FAIR) / TOTAL_MEM) / (TOTAL_MEM - 1)
    d2 = SMOOTH_WIDTH * SMOOTH_WIDTH

    def pairwise(q):
        mine_r, mine_l = me // NL, me % NL
        lanes = ds(q * CQ + mine_l * 128, 128, 128)
        mean = jnp.sum(jnp.sum(av[...], axis=0), keepdims=True) / TOTAL_CELLS
        area = aw[pl.ds(q * NL + mine_l, 1), :] / mean

        def tile(rows, n):
            scale = area * vcol[mine_r, rows, :]
            t = tgt[mine_r, rows, lanes]
            f = [fr[q, k // 2, k % 2, rows, :] for k in range(TOTAL_MEM)]
            s = [None] * TOTAL_MEM
            spread = None
            for i in range(TOTAL_MEM):
                for k in range(i + 1, TOTAL_MEM):
                    d = f[i] - f[k]
                    w = d * d + d2
                    inv = lax.rsqrt(w)
                    slope = d * inv
                    s[i] = slope if s[i] is None else s[i] + slope
                    s[k] = -slope if s[k] is None else s[k] - slope
                    smooth = w * inv - SMOOTH_WIDTH
                    spread = smooth if spread is None else spread + smooth
            truth = None
            for i in range(TOTAL_MEM):
                d = f[i] - t
                w = d * d + d2
                inv = lax.rsqrt(w)
                gs[q, i // 2, i % 2, rows, :] = scale * (d * inv - coef * s[i])
                smooth = w * inv - SMOOTH_WIDTH
                truth = smooth if truth is None else truth + smooth
            loss[0:n, :] += scale * (truth / TOTAL_MEM - (coef / TOTAL_MEM) * spread)

        for i in range(0, VH, 8):
            tile(pl.ds(i, min(8, VH - i)), min(8, VH - i))

    def backward(q):
        sl = pl.ds(q * CQ, CQ)
        gap = jnp.zeros((VG - VH, 128), F32)

        for m in range(MEM):
            for l in range(NL):
                groups = []
                for r in range(NR):
                    groups += [gr[q, r * NL + l, m], gap]
                at = q * CQ + 128 * l
                gv[m, :, at : at + 128] = jnp.concatenate(groups, axis=0).astype(BF16)
            gp[m, :, sl] = (dot(w2p[...], gv[m, :, sl]) * dg[m, :, sl]).astype(BF16)

    def add_to_grad(rows, cols, new, first):
        if first:
            grad[rows, cols] = new
        else:
            grad[rows, cols] += new

    def grad_in_tile(sl, half, j, first):
        rows, cols = ds(half * HALF, HALF, HALF), ds(j * 256, 256, 256)
        new = dot_t(e[0, rows, sl], gp[0, cols, sl]) + dot_t(e[1, rows, sl], gp[1, cols, sl])
        add_to_grad(rows, cols, new, first)

    def grad_out_tile(sl, half, first):
        rows = ds(half * HALF, HALF, HALF)
        new = dot_t(act[0, rows, sl], gv[0, :, sl]) + dot_t(act[1, rows, sl], gv[1, :, sl])
        add_to_grad(rows, pl.ds(H, VP), new, first)

    def weight_gradients(q, n, half):
        sl = pl.ds(q * CQ, n * CQ)

        for j in range(4):
            grad_in_tile(sl, half, j, q == 0)

        grad_out_tile(sl, half, q == 0)

    def embedding_derivative(m, q):
        sl = pl.ds(q * 512, 512)
        ed[m, :, sl] = dot(w1[...], gp[m, :, sl]).astype(BF16)

    def cols_of(u):
        return pl.ds(u * 128, 128)

    def along(u, level, s):
        return (pos[ORDERS[u % 3][level]] + s) % 4

    def peer_of(u, level, s):
        return device(moved(**{ORDERS[u % 3][level]: s}))

    def block_rows(ks):
        begin = core * HALF
        for k, size in zip(ks, (128, 32)):
            begin = begin + k * size
        size = (128, 32)[len(ks) - 1]
        return ds(begin, size, size)

    def core_send(u):
        remote(
            grad.at[ds((1 - core) * HALF, HALF, HALF), cols_of(u)], core_in.at[:, cols_of(u)],
            core_sem.at[NU], core_sem.at[u], other_core,
        ).start()

    def core_receive(u):
        cols = cols_of(u)
        arrived(core_in.at[:, cols], core_sem.at[u])
        grad[ds(core * HALF, HALF, HALF), cols] += core_in[:, cols]
        for s in OFFSETS:
            k = along(u, 0, s)
            remote(
                grad.at[block_rows([k]), cols], s1.at[u, s - 1],
                rs0_sem.at[NU], rs0_sem.at[u], peer_of(u, 0, s),
            ).start()

    def rs0_receive(u):
        arrived(s1.at[u], rs0_sem.at[u])
        own = grad[block_rows([along(u, 0, 0)]), cols_of(u)]
        r1[u] = own + s1[u, 0] + s1[u, 1] + s1[u, 2]
        for s in OFFSETS:
            k = along(u, 1, s)
            remote(
                r1.at[u, ds(k * 32, 32, 32)], s2.at[u, s - 1],
                rs1_sem.at[NU], rs1_sem.at[u], peer_of(u, 1, s),
            ).start()

    def rs1_receive(u):
        arrived(s2.at[u], rs1_sem.at[u])
        own = r1[u, ds(along(u, 1, 0) * 32, 32, 32)]
        k = along(u, 2, 0)
        s3[u, k] = own + s2[u, 0] + s2[u, 1] + s2[u, 2]
        for s in OFFSETS:
            remote(
                s3.at[u, k], s3.at[u, k], x_sem.at[NU], x_sem.at[u], peer_of(u, 2, s)
            ).start()

    rescale = 1.0 / math.sqrt(TOTAL_MEM * TOTAL_CELLS)

    def x_receive(u):
        arrived(s3.at[u, pl.ds(0, 3)], x_sem.at[u])
        at = (block_rows([along(u, 0, 0), along(u, 1, 0)]), cols_of(u))
        full[at] = (s3[u, 0] + s3[u, 1] + s3[u, 2] + s3[u, 3]) * rescale
        for s in OFFSETS:
            remote(
                full.at[at], full.at[at], ag1_sem.at[NU], ag1_sem.at[u], peer_of(u, 1, s)
            ).start()

    def to_core(u, s):
        at = (block_rows([along(u, 0, s)]), cols_of(u))
        remote(full.at[at], full.at[at], cg_sem.at[NU], cg_sem.at[u], other_core).start()

    def ag1_receive(u):
        arrived(full.at[pl.ds(0, 96), cols_of(u)], ag1_sem.at[u])
        at = (block_rows([along(u, 0, 0)]), cols_of(u))
        for s in OFFSETS:
            remote(
                full.at[at], full.at[at], ag0_sem.at[NU], ag0_sem.at[u], peer_of(u, 0, s)
            ).start()
        to_core(u, 0)

    def ag0_receive(u):
        arrived(full.at[pl.ds(0, 384), cols_of(u)], ag0_sem.at[u])
        for s in OFFSETS:
            to_core(u, s)

    def cg_receive(u):
        arrived(full.at[pl.ds(0, HALF), cols_of(u)], cg_sem.at[u])

    def run():
        load()
        greet()
        small_operands()
        w1_copy.wait()
        w1t[...] = w1[...].T
        forward(0, (0,))
        pl.semaphore_wait(barrier, 23)
        send_member(0, 0)
        forward(0, (1,))
        send_member(0, 1)
        send_area()
        forward(1)
        send_all(1, fs, fr, f_sem)
        forward(2)
        send_all(2, fs, fr, f_sem)
        arrived(av.at[pl.ds(0, 15)], area_sem.at[1])
        receive_all(0, fr, f_sem)
        pairwise(0)
        send_all(0, gs, gr, g_sem)
        forward(3)
        send_all(3, fs, fr, f_sem)
        receive_all(1, fr, f_sem)
        pairwise(1)
        send_all(1, gs, gr, g_sem)
        receive_all(2, fr, f_sem)
        pairwise(2)
        send_all(2, gs, gr, g_sem)
        receive_all(0, gr, g_sem)
        backward(0)
        receive_all(3, fr, f_sem)
        pairwise(3)
        send_all(3, gs, gr, g_sem)
        receive_all(1, gr, g_sem)
        backward(1)
        weight_gradients(0, 2, 0)
        weight_gradients(0, 2, 1)
        receive_all(2, gr, g_sem)
        backward(2)
        receive_all(3, gr, g_sem)
        backward(3)
        own_loss = jnp.sum(loss[...], keepdims=True)
        row = lax.broadcasted_iota(jnp.int32, (8, VP), 0)
        col = lax.broadcasted_iota(jnp.int32, (8, VP), 1)
        grad[0:8, H:WIDE] += jnp.where((row == 0) & (col == LOSS_COL), own_loss, 0.0)
        last = pl.ds(2 * CQ, 2 * CQ)
        for j in range(4):
            grad_in_tile(last, 1 - core, j, False)
            core_send(2 * j)
            core_send(2 * j + 1)
        grad_out_tile(last, 1 - core, False)
        core_send(NU - 1)
        grad_in_tile(last, core, 0, False)
        core_receive(0)
        grad_in_tile(last, core, 1, False)
        core_receive(1)
        grad_in_tile(last, core, 2, False)
        core_receive(2)
        core_receive(3)
        grad_in_tile(last, core, 3, False)
        core_receive(4)
        grad_out_tile(last, core, False)
        core_receive(5)
        waves = ((0, 1, 2), (3, 4, 5), (6, 7, 8))

        def each(step, wave):
            for u in waves[wave]:
                step(u)

        embedding_derivative(0, 0)
        each(rs0_receive, 0)
        each(core_receive, 2)
        embedding_derivative(1, 0)
        each(rs0_receive, 1)
        each(rs1_receive, 0)
        each(rs0_receive, 2)
        each(rs1_receive, 1)
        each(x_receive, 0)
        each(rs1_receive, 2)
        each(x_receive, 1)
        each(ag1_receive, 0)
        each(x_receive, 2)
        each(ag1_receive, 1)
        each(ag1_receive, 2)
        embedding_derivative(0, 1)
        each(ag0_receive, 0)
        embedding_derivative(1, 1)
        each(ag0_receive, 1)
        each(ag0_receive, 2)
        for wave in range(3):
            each(cg_receive, wave)

    run()
    left(av.at[pl.ds(0, 15)], area_sem.at[0])
    left(fs.at[:, pl.ds(0, 7)], f_sem.at[NQ])
    left(gs.at[:, pl.ds(0, 7)], g_sem.at[NQ])
    left(core_in, core_sem.at[NU])
    left(s1, rs0_sem.at[NU])
    left(s2, rs1_sem.at[NU])
    left(s3.at[:, pl.ds(0, 3)], x_sem.at[NU])
    left(s2, ag1_sem.at[NU])
    left(s1, ag0_sem.at[NU])
    left(core_in, cg_sem.at[NU])


def finish(ed, full, ed_out, grad_out, grad_t_out, penalty, sem):
    ed_copy = pltpu.make_async_copy(ed, ed_out, sem.at[0])
    ed_copy.start()
    grad_copy = pltpu.make_async_copy(full.at[:, 0:H], grad_out, sem.at[1])
    grad_copy.start()
    t = full[:, H:WIDE].T
    grad_t_out[...] = jnp.concatenate([t[VG * r : VG * r + VH] for r in range(NR)], axis=0)
    rescale = 1.0 / math.sqrt(TOTAL_MEM * TOTAL_CELLS)
    at = full[0:1, H + LOSS_COL : H + LOSS_COL + 1]
    penalty[...] = at * (1.0 / (rescale * TOTAL_CELLS * V))
    ed_copy.wait()
    grad_copy.wait()


def per_device(
    embedding_tensor,
    first_projection_matrix,
    variable_projection_matrix,
    target,
    var_weight,
    area_weight,
):
    vmem = pl.BlockSpec(memory_space=pltpu.VMEM)
    hbm = pl.BlockSpec(memory_space=pl.ANY)
    dma = pltpu.SemaphoreType.DMA
    big = (MEM, H, CELLS)
    swap = (NQ, 8, MEM, VH, 128)
    in_vmem = (pltpu.VMEM(big, BF16), pltpu.VMEM((H, WIDE), F32))
    ed, full = pl.pallas_call(
        kernel,
        name="decoder_crps",
        out_shape=in_vmem,
        in_specs=[hbm] * 6,
        out_specs=(vmem, vmem),
        scratch_shapes=[
            pltpu.VMEM(big, BF16),
            pltpu.VMEM((H, H), BF16),
            pltpu.VMEM((H, H), BF16),
            pltpu.VMEM((V, H), BF16),
            pltpu.VMEM((V, CELLS), BF16),
            pltpu.VMEM((1, V), F32),
            pltpu.VMEM((8, 128), F32),
            pltpu.VMEM((H, VP), BF16),
            pltpu.VMEM((VP, H), BF16),
            pltpu.VMEM(big, BF16),
            pltpu.VMEM(big, F32),
            pltpu.VMEM((MEM, VP, CELLS), BF16),
            pltpu.VMEM(big, BF16),
            pltpu.VMEM((NR, VH, CELLS), F32),
            pltpu.VMEM((NR, VH, 128), F32),
            pltpu.VMEM((16, 8, 128), F32),
            pltpu.VMEM(swap, F32),
            pltpu.VMEM(swap, F32),
            pltpu.VMEM(swap, F32),
            pltpu.VMEM(swap, F32),
            pltpu.VMEM((H, WIDE), F32),
            pltpu.VMEM((HALF, WIDE), F32),
            pltpu.VMEM((NU, 3, 128, 128), F32),
            pltpu.VMEM((NU, 128, 128), F32),
            pltpu.VMEM((NU, 3, 32, 128), F32),
            pltpu.VMEM((NU, 4, 32, 128), F32),
            pltpu.VMEM((8, 128), F32),
            dma((NQ + 5,)),
            dma((2,)),
            dma((NQ + 1,)), dma((NQ + 1,)),
            dma((NU + 1,)), dma((NU + 1,)), dma((NU + 1,)), dma((NU + 1,)),
            dma((NU + 1,)), dma((NU + 1,)), dma((NU + 1,)),
        ],
        compiler_params=pltpu.CompilerParams(
            collective_id=0, has_side_effects=True, vmem_limit_bytes=50 * 2**20
        ),
        cost_estimate=pl.CostEstimate(
            flops=15_000_000_000, bytes_accessed=20_000_000, transcendentals=4_000_000
        ),
    )(
        embedding_tensor,
        first_projection_matrix,
        variable_projection_matrix.T,
        target,
        var_weight.reshape(1, V),
        area_weight.reshape(8, 128),
    )
    ed, grad_in, grad_out_t, penalty = pl.pallas_call(
        finish,
        name="write_out",
        out_shape=(
            jax.ShapeDtypeStruct(big, BF16),
            jax.ShapeDtypeStruct((H, H), F32),
            jax.ShapeDtypeStruct((V, H), F32),
            jax.ShapeDtypeStruct((1, 1), F32),
        ),
        in_specs=[vmem, vmem],
        out_specs=(hbm, hbm, vmem, vmem),
        scratch_shapes=[dma((2,))],
        compiler_params=pltpu.CompilerParams(vmem_limit_bytes=8 * 2**20),
    )(ed, full)
    return ed, grad_in, grad_out_t.T, penalty[0, 0]


def solution(mesh):
    in_specs = (P("member", None, "grid"), P(), P(), P(None, "grid"), P(), P("grid"))
    out_specs = (P("member", None, "grid"), P(), P(), P())
    return jax.shard_map(
        per_device, mesh=mesh, in_specs=in_specs, out_specs=out_specs, check_vma=False
    )
```

```python
import functools
import math

import jax
import jax.numpy as jnp
from jax import lax
from jax.experimental import pallas as pl
from jax.experimental.pallas import tpu as pltpu
from jax.sharding import PartitionSpec as P

SMOOTH_WIDTH = 0.1
ALPHA_FAIR = 0.95
MESH = pl.DeviceIdType.MESH
F32 = jnp.float32
BF16 = jnp.bfloat16
GELU_A = math.sqrt(2.0 / math.pi)
GELU_B = 0.044715

H = 1024
V = 100
CELLS = 1024
MEM = 2
TOTAL_MEM = 16
TOTAL_CELLS = 16384
NQ = 4
CQ = CELLS // NQ
NL = CQ // 128
NR = 8 // NL
VH = V // NR
VG = 128 // NR
VP = NR * VG
HALF = H // 2
WIDE = H + VP
NU = WIDE // 128
LOSS_COL = VH
ORDERS = (("x", "y", "z"), ("y", "z", "x"), ("z", "x", "y"))
OFFSETS = (2, 1, 3)


def dot(a, b):
    return lax.dot_general(a, b, (((1,), (0,)), ((), ())), preferred_element_type=F32)


def dot_t(a, b):
    return lax.dot_general(a, b, (((1,), (1,)), ((), ())), preferred_element_type=F32)


def gelu_and_derivative(x):
    x2 = x * x
    t = jnp.tanh(x * (GELU_A + (GELU_A * GELU_B) * x2))
    h = 0.5 + 0.5 * t
    y = x * h
    return y, h + (y * (1.0 - t)) * (GELU_A + (3.0 * GELU_A * GELU_B) * x2)


def ds(start, size, multiple):
    return pl.ds(pl.multiple_of(start, multiple), size)


def kernel(
    emb, w1_hbm, w2_hbm, target_hbm, vw_hbm, aw_hbm,
    ed, full,
    e, w1, w1t, w2_in, target, vw, aw, w2p, w2t, act, dg, gv, gp, tgt, vcol, av,
    fs, fr, gs, gr, grad, core_in, s1, r1, s2, s3, loss,
    in_sem, area_sem, f_sem, g_sem, core_sem, rs0_sem, rs1_sem, x_sem, ag1_sem, ag0_sem, cg_sem,
):
    me = lax.axis_index("member")
    g = lax.axis_index("grid")
    pos = {"x": me % 4, "y": (g // 8) * 2 + me // 4, "z": (g // 2) % 4, "c": g % 2}
    core = pos["c"]

    def device(p):
        return ((p["y"] % 2) * 4 + p["x"], ((p["y"] // 2) * 4 + p["z"]) * 2 + p["c"])

    def moved(**by):
        return {k: (v + by[k]) % (2 if k == "c" else 4) if k in by else v for k, v in pos.items()}

    def remote(src, dst, send_sem, recv_sem, to):
        return pltpu.make_async_remote_copy(
            src_ref=src, dst_ref=dst, send_sem=send_sem, recv_sem=recv_sem,
            device_id=to, device_id_type=MESH,
        )

    other_core = device(moved(c=1))

    def arrived(ref, sem):
        remote(ref, ref, sem, sem, other_core).wait_recv()

    def left(ref, sem):
        remote(ref, ref, sem, sem, other_core).wait_send()

    def member_peer(o):
        return (me // 4 + o // 4) % 2 * 4 + (me % 4 + o % 4) % 4

    def emb_copy(q):
        sl = pl.ds(q * CQ, CQ)
        return pltpu.make_async_copy(emb.at[:, :, sl], e.at[:, :, sl], in_sem.at[q])

    w1_copy = pltpu.make_async_copy(w1_hbm, w1, in_sem.at[NQ])
    small_copies = [
        pltpu.make_async_copy(src, dst, in_sem.at[NQ + 1 + i])
        for i, (src, dst) in enumerate(
            ((w2_hbm, w2_in), (target_hbm, target), (vw_hbm, vw), (aw_hbm, aw))
        )
    ]
    barrier = pltpu.get_barrier_semaphore()

    def load():
        for copy in small_copies:
            copy.start()
        w1_copy.start()
        for q in range(NQ):
            emb_copy(q).start()

    def greet():
        peers = [(member_peer(o), g) for o in range(1, 8)]
        peers += [(me, (g + o) % 16) for o in range(1, 16)]
        peers += [((me + 4) % 8, (g + 8) % 16)]
        for peer in peers:
            pl.semaphore_signal(barrier, inc=1, device_id=peer, device_id_type=MESH)

    def small_operands():
        for copy in small_copies:
            copy.wait()
        wide = w2_in[...].astype(F32)
        gap = jnp.zeros((VG - VH, H), F32)
        groups = []
        for r in range(NR):
            groups += [wide[r * VH : r * VH + VH], gap]
        w2t[...] = jnp.concatenate(groups, axis=0).astype(BF16)
        w2p[...] = w2t[...].T
        t32 = target[...].astype(F32)
        columns = jnp.broadcast_to(vw[...], (128, V)).T
        for r in range(NR):
            tgt[r] = t32[r * VH : r * VH + VH]
            vcol[r] = columns[r * VH : r * VH + VH]
        av[g] = aw[...]
        loss[...] = jnp.zeros_like(loss)

    def send_area():
        for o in range(1, 16):
            remote(
                av.at[g], av.at[g], area_sem.at[0], area_sem.at[1], (me, (g + o) % 16)
            ).start()

    PEERS = (6, 2, 5, 7, 4, 1, 3)

    def send_all(q, src, dst, sem):
        for o in PEERS:
            peer = member_peer(o)
            remote(src.at[q, peer], dst.at[q, me], sem.at[NQ], sem.at[q], (peer, g)).start()
        dst[q, me] = src[q, me]

    def receive_all(q, dst, sem):
        arrived(dst.at[q, pl.ds(0, 7)], sem.at[q])

    def send_member(q, m):
        for o in PEERS:
            peer = member_peer(o)
            remote(
                fs.at[q, peer, m], fr.at[q, me, m], f_sem.at[NQ], f_sem.at[q], (peer, g)
            ).start()
        fr[q, me, m] = fs[q, me, m]

    def forward(q, members=range(MEM)):
        sl = pl.ds(q * CQ, CQ)
        if 0 in members:
            emb_copy(q).wait()
        for m in members:
            y, d = gelu_and_derivative(dot(w1t[...], e[m, :, sl]))
            act[m, :, sl] = y.astype(BF16)
            dg[m, :, sl] = d
            fc = dot(w2t[...], act[m, :, sl])
            for r in range(NR):
                for l in range(NL):
                    fs[q, r * NL + l, m] = fc[VG * r : VG * r + VH, 128 * l : 128 * l + 128]

    coef = (1.0 - (1.0 - ALPHA_FAIR) / TOTAL_MEM) / (TOTAL_MEM - 1)
    d2 = SMOOTH_WIDTH * SMOOTH_WIDTH

    def pairwise(q):
        mine_r, mine_l = me // NL, me % NL
        lanes = ds(q * CQ + mine_l * 128, 128, 128)
        mean = jnp.sum(jnp.sum(av[...], axis=0), keepdims=True) / TOTAL_CELLS
        area = aw[pl.ds(q * NL + mine_l, 1), :] / mean

        def tile(rows, n):
            scale = area * vcol[mine_r, rows, :]
            t = tgt[mine_r, rows, lanes]
            f = [fr[q, k // 2, k % 2, rows, :] for k in range(TOTAL_MEM)]
            s = [None] * TOTAL_MEM
            spread = None
            for i in range(TOTAL_MEM):
                for k in range(i + 1, TOTAL_MEM):
                    d = f[i] - f[k]
                    w = d * d + d2
                    inv = lax.rsqrt(w)
                    slope = d * inv
                    s[i] = slope if s[i] is None else s[i] + slope
                    s[k] = -slope if s[k] is None else s[k] - slope
                    smooth = w * inv - SMOOTH_WIDTH
                    spread = smooth if spread is None else spread + smooth
            truth = None
            for i in range(TOTAL_MEM):
                d = f[i] - t
                w = d * d + d2
                inv = lax.rsqrt(w)
                gs[q, i // 2, i % 2, rows, :] = scale * (d * inv - coef * s[i])
                smooth = w * inv - SMOOTH_WIDTH
                truth = smooth if truth is None else truth + smooth
            loss[0:n, :] += scale * (truth / TOTAL_MEM - (coef / TOTAL_MEM) * spread)

        for i in range(0, VH, 8):
            tile(pl.ds(i, min(8, VH - i)), min(8, VH - i))

    def backward(q):
        sl = pl.ds(q * CQ, CQ)
        gap = jnp.zeros((VG - VH, 128), F32)

        for m in range(MEM):
            for l in range(NL):
                groups = []
                for r in range(NR):
                    groups += [gr[q, r * NL + l, m], gap]
                at = q * CQ + 128 * l
                gv[m, :, at : at + 128] = jnp.concatenate(groups, axis=0).astype(BF16)
            gp[m, :, sl] = (dot(w2p[...], gv[m, :, sl]) * dg[m, :, sl]).astype(BF16)

    def add_to_grad(rows, cols, new, first):
        if first:
            grad[rows, cols] = new
        else:
            grad[rows, cols] += new

    def grad_in_tile(sl, half, j, first):
        rows, cols = ds(half * HALF, HALF, HALF), ds(j * 256, 256, 256)
        new = dot_t(e[0, rows, sl], gp[0, cols, sl]) + dot_t(e[1, rows, sl], gp[1, cols, sl])
        add_to_grad(rows, cols, new, first)

    def grad_out_tile(sl, half, first):
        rows = ds(half * HALF, HALF, HALF)
        new = dot_t(act[0, rows, sl], gv[0, :, sl]) + dot_t(act[1, rows, sl], gv[1, :, sl])
        add_to_grad(rows, pl.ds(H, VP), new, first)

    def weight_gradients(q, n, half):
        sl = pl.ds(q * CQ, n * CQ)

        for j in range(4):
            grad_in_tile(sl, half, j, q == 0)

        grad_out_tile(sl, half, q == 0)

    def embedding_derivative(m, q):
        sl = pl.ds(q * 512, 512)
        ed[m, :, sl] = dot(w1[...], gp[m, :, sl]).astype(BF16)

    def cols_of(u):
        return pl.ds(u * 128, 128)

    def along(u, level, s):
        return (pos[ORDERS[u % 3][level]] + s) % 4

    def peer_of(u, level, s):
        return device(moved(**{ORDERS[u % 3][level]: s}))

    def block_rows(ks):
        begin = core * HALF
        for k, size in zip(ks, (128, 32)):
            begin = begin + k * size
        size = (128, 32)[len(ks) - 1]
        return ds(begin, size, size)

    def core_send(u):
        remote(
            grad.at[ds((1 - core) * HALF, HALF, HALF), cols_of(u)], core_in.at[:, cols_of(u)],
            core_sem.at[NU], core_sem.at[u], other_core,
        ).start()

    def core_receive(u):
        cols = cols_of(u)
        arrived(core_in.at[:, cols], core_sem.at[u])
        grad[ds(core * HALF, HALF, HALF), cols] += core_in[:, cols]
        for s in OFFSETS:
            k = along(u, 0, s)
            remote(
                grad.at[block_rows([k]), cols], s1.at[u, s - 1],
                rs0_sem.at[NU], rs0_sem.at[u], peer_of(u, 0, s),
            ).start()

    def rs0_receive(u):
        arrived(s1.at[u], rs0_sem.at[u])
        own = grad[block_rows([along(u, 0, 0)]), cols_of(u)]
        r1[u] = own + s1[u, 0] + s1[u, 1] + s1[u, 2]
        for s in OFFSETS:
            k = along(u, 1, s)
            remote(
                r1.at[u, ds(k * 32, 32, 32)], s2.at[u, s - 1],
                rs1_sem.at[NU], rs1_sem.at[u], peer_of(u, 1, s),
            ).start()

    def rs1_receive(u):
        arrived(s2.at[u], rs1_sem.at[u])
        own = r1[u, ds(along(u, 1, 0) * 32, 32, 32)]
        k = along(u, 2, 0)
        s3[u, k] = own + s2[u, 0] + s2[u, 1] + s2[u, 2]
        for s in OFFSETS:
            remote(
                s3.at[u, k], s3.at[u, k], x_sem.at[NU], x_sem.at[u], peer_of(u, 2, s)
            ).start()

    rescale = 1.0 / math.sqrt(TOTAL_MEM * TOTAL_CELLS)

    def x_receive(u):
        arrived(s3.at[u, pl.ds(0, 3)], x_sem.at[u])
        at = (block_rows([along(u, 0, 0), along(u, 1, 0)]), cols_of(u))
        full[at] = (s3[u, 0] + s3[u, 1] + s3[u, 2] + s3[u, 3]) * rescale
        for s in OFFSETS:
            remote(
                full.at[at], full.at[at], ag1_sem.at[NU], ag1_sem.at[u], peer_of(u, 1, s)
            ).start()

    def to_core(u, s):
        at = (block_rows([along(u, 0, s)]), cols_of(u))
        remote(full.at[at], full.at[at], cg_sem.at[1], cg_sem.at[0], other_core).start()

    def ag1_receive(u):
        arrived(full.at[pl.ds(0, 96), cols_of(u)], ag1_sem.at[u])
        at = (block_rows([along(u, 0, 0)]), cols_of(u))
        for s in OFFSETS:
            sem = ag0_sem.at[u if u < NU - 3 else single(u, s)]
            remote(full.at[at], full.at[at], ag0_sem.at[NU], sem, peer_of(u, 0, s)).start()
        to_core(u, 0)

    def ag0_receive(u):
        arrived(full.at[pl.ds(0, 384), cols_of(u)], ag0_sem.at[u])
        for s in OFFSETS:
            to_core(u, s)

    def single(u, s):
        return NU + 1 + (u - (NU - 3)) * 3 + s - 1

    def ag0_receive_block(u, s):
        at = full.at[block_rows([along(u, 0, 4 - s)]), cols_of(u)]
        arrived(at, ag0_sem.at[single(u, s)])
        to_core(u, 4 - s)

    def run():
        load()
        greet()
        small_operands()
        w1_copy.wait()
        w1t[...] = w1[...].T
        forward(0, (0,))
        pl.semaphore_wait(barrier, 23)
        send_member(0, 0)
        forward(0, (1,))
        send_member(0, 1)
        send_area()
        forward(1)
        send_all(1, fs, fr, f_sem)
        forward(2)
        send_all(2, fs, fr, f_sem)
        arrived(av.at[pl.ds(0, 15)], area_sem.at[1])
        receive_all(0, fr, f_sem)
        pairwise(0)
        send_all(0, gs, gr, g_sem)
        forward(3)
        send_all(3, fs, fr, f_sem)
        receive_all(1, fr, f_sem)
        pairwise(1)
        send_all(1, gs, gr, g_sem)
        receive_all(2, fr, f_sem)
        pairwise(2)
        send_all(2, gs, gr, g_sem)
        receive_all(0, gr, g_sem)
        backward(0)
        receive_all(3, fr, f_sem)
        pairwise(3)
        send_all(3, gs, gr, g_sem)
        receive_all(1, gr, g_sem)
        backward(1)
        weight_gradients(0, 2, 0)
        weight_gradients(0, 2, 1)
        receive_all(2, gr, g_sem)
        backward(2)
        receive_all(3, gr, g_sem)
        backward(3)
        own_loss = jnp.sum(loss[...], keepdims=True)
        row = lax.broadcasted_iota(jnp.int32, (8, VP), 0)
        col = lax.broadcasted_iota(jnp.int32, (8, VP), 1)
        grad[0:8, H:WIDE] += jnp.where((row == 0) & (col == LOSS_COL), own_loss, 0.0)
        last = pl.ds(2 * CQ, 2 * CQ)
        for j in range(4):
            grad_in_tile(last, 1 - core, j, False)
            core_send(2 * j)
            core_send(2 * j + 1)
        grad_out_tile(last, 1 - core, False)
        core_send(NU - 1)
        grad_in_tile(last, core, 0, False)
        core_receive(0)
        grad_in_tile(last, core, 1, False)
        core_receive(1)
        grad_in_tile(last, core, 2, False)
        core_receive(2)
        core_receive(3)
        grad_in_tile(last, core, 3, False)
        core_receive(4)
        grad_out_tile(last, core, False)
        core_receive(5)
        waves = ((0, 1, 2), (3, 4, 5), (6, 7, 8))

        def each(step, wave):
            for u in waves[wave]:
                step(u)

        embedding_derivative(0, 0)
        each(rs0_receive, 0)
        each(core_receive, 2)
        embedding_derivative(1, 0)
        each(rs0_receive, 1)
        each(rs1_receive, 0)
        embedding_derivative(0, 1)
        each(rs0_receive, 2)
        each(rs1_receive, 1)
        each(x_receive, 0)
        each(rs1_receive, 2)
        each(x_receive, 1)
        each(ag1_receive, 0)
        each(x_receive, 2)
        embedding_derivative(1, 1)
        each(ag1_receive, 1)
        each(ag1_receive, 2)
        each(ag0_receive, 0)
        each(ag0_receive, 1)
        for s in (1, 3, 2):
            for u in waves[2]:
                ag0_receive_block(u, s)
        arrived(full.at[pl.ds(0, HALF)], cg_sem.at[0])

    run()
    left(av.at[pl.ds(0, 15)], area_sem.at[0])
    left(fs.at[:, pl.ds(0, 7)], f_sem.at[NQ])
    left(gs.at[:, pl.ds(0, 7)], g_sem.at[NQ])
    left(core_in, core_sem.at[NU])
    left(s1, rs0_sem.at[NU])
    left(s2, rs1_sem.at[NU])
    left(s3.at[:, pl.ds(0, 3)], x_sem.at[NU])
    left(s2, ag1_sem.at[NU])
    left(s1, ag0_sem.at[NU])
    left(core_in, cg_sem.at[1])


def finish(ed, full, ed_out, grad_out, grad_t_out, penalty, sem):
    ed_copy = pltpu.make_async_copy(ed, ed_out, sem.at[0])
    ed_copy.start()
    grad_copy = pltpu.make_async_copy(full.at[:, 0:H], grad_out, sem.at[1])
    grad_copy.start()
    t = full[:, H:WIDE].T
    grad_t_out[...] = jnp.concatenate([t[VG * r : VG * r + VH] for r in range(NR)], axis=0)
    rescale = 1.0 / math.sqrt(TOTAL_MEM * TOTAL_CELLS)
    at = full[0:1, H + LOSS_COL : H + LOSS_COL + 1]
    penalty[...] = at * (1.0 / (rescale * TOTAL_CELLS * V))
    ed_copy.wait()
    grad_copy.wait()


def per_device(
    embedding_tensor,
    first_projection_matrix,
    variable_projection_matrix,
    target,
    var_weight,
    area_weight,
):
    vmem = pl.BlockSpec(memory_space=pltpu.VMEM)
    hbm = pl.BlockSpec(memory_space=pl.ANY)
    dma = pltpu.SemaphoreType.DMA
    big = (MEM, H, CELLS)
    swap = (NQ, 8, MEM, VH, 128)
    in_vmem = (pltpu.VMEM(big, BF16), pltpu.VMEM((H, WIDE), F32))
    ed, full = pl.pallas_call(
        kernel,
        name="decoder_crps",
        out_shape=in_vmem,
        in_specs=[hbm] * 6,
        out_specs=(vmem, vmem),
        scratch_shapes=[
            pltpu.VMEM(big, BF16),
            pltpu.VMEM((H, H), BF16),
            pltpu.VMEM((H, H), BF16),
            pltpu.VMEM((V, H), BF16),
            pltpu.VMEM((V, CELLS), BF16),
            pltpu.VMEM((1, V), F32),
            pltpu.VMEM((8, 128), F32),
            pltpu.VMEM((H, VP), BF16),
            pltpu.VMEM((VP, H), BF16),
            pltpu.VMEM(big, BF16),
            pltpu.VMEM(big, F32),
            pltpu.VMEM((MEM, VP, CELLS), BF16),
            pltpu.VMEM(big, BF16),
            pltpu.VMEM((NR, VH, CELLS), F32),
            pltpu.VMEM((NR, VH, 128), F32),
            pltpu.VMEM((16, 8, 128), F32),
            pltpu.VMEM(swap, F32),
            pltpu.VMEM(swap, F32),
            pltpu.VMEM(swap, F32),
            pltpu.VMEM(swap, F32),
            pltpu.VMEM((H, WIDE), F32),
            pltpu.VMEM((HALF, WIDE), F32),
            pltpu.VMEM((NU, 3, 128, 128), F32),
            pltpu.VMEM((NU, 128, 128), F32),
            pltpu.VMEM((NU, 3, 32, 128), F32),
            pltpu.VMEM((NU, 4, 32, 128), F32),
            pltpu.VMEM((8, 128), F32),
            dma((NQ + 5,)),
            dma((2,)),
            dma((NQ + 1,)), dma((NQ + 1,)),
            dma((NU + 1,)), dma((NU + 1,)), dma((NU + 1,)), dma((NU + 1,)),
            dma((NU + 1,)), dma((NU + 10,)), dma((2,)),
        ],
        compiler_params=pltpu.CompilerParams(
            collective_id=0, has_side_effects=True, vmem_limit_bytes=50 * 2**20
        ),
        cost_estimate=pl.CostEstimate(
            flops=15_000_000_000, bytes_accessed=20_000_000, transcendentals=4_000_000
        ),
    )(
        embedding_tensor,
        first_projection_matrix,
        variable_projection_matrix.T,
        target,
        var_weight.reshape(1, V),
        area_weight.reshape(8, 128),
    )
    ed, grad_in, grad_out_t, penalty = pl.pallas_call(
        finish,
        name="write_out",
        out_shape=(
            jax.ShapeDtypeStruct(big, BF16),
            jax.ShapeDtypeStruct((H, H), F32),
            jax.ShapeDtypeStruct((V, H), F32),
            jax.ShapeDtypeStruct((1, 1), F32),
        ),
        in_specs=[vmem, vmem],
        out_specs=(hbm, hbm, vmem, vmem),
        scratch_shapes=[dma((2,))],
        compiler_params=pltpu.CompilerParams(vmem_limit_bytes=8 * 2**20),
    )(ed, full)
    return ed, grad_in, grad_out_t.T, penalty[0, 0]


def solution(mesh):
    in_specs = (P("member", None, "grid"), P(), P(), P(None, "grid"), P(), P("grid"))
    out_specs = (P("member", None, "grid"), P(), P(), P())
    return jax.shard_map(
        per_device, mesh=mesh, in_specs=in_specs, out_specs=out_specs, check_vma=False
    )
```

```python
import functools
import math

import jax
import jax.numpy as jnp
from jax import lax
from jax.experimental import pallas as pl
from jax.experimental.pallas import tpu as pltpu
from jax.sharding import PartitionSpec as P

SMOOTH_WIDTH = 0.1
ALPHA_FAIR = 0.95
MESH = pl.DeviceIdType.MESH
F32 = jnp.float32
BF16 = jnp.bfloat16
GELU_A = math.sqrt(2.0 / math.pi)
GELU_B = 0.044715

H = 1024
V = 100
CELLS = 1024
MEM = 2
TOTAL_MEM = 16
TOTAL_CELLS = 16384
NQ = 4
CQ = CELLS // NQ
NL = CQ // 128
NR = 8 // NL
VH = V // NR
VG = 128 // NR
VP = NR * VG
HALF = H // 2
WIDE = H + VP
NU = WIDE // 128
LOSS_COL = VH
ORDERS = (("x", "y", "z"), ("y", "z", "x"), ("z", "x", "y"))
OFFSETS = (2, 1, 3)


def dot(a, b):
    return lax.dot_general(a, b, (((1,), (0,)), ((), ())), preferred_element_type=F32)


def dot_t(a, b):
    return lax.dot_general(a, b, (((1,), (1,)), ((), ())), preferred_element_type=F32)


def gelu_and_derivative(x):
    x2 = x * x
    t = jnp.tanh(x * (GELU_A + (GELU_A * GELU_B) * x2))
    h = 0.5 + 0.5 * t
    y = x * h
    return y, h + (y * (1.0 - t)) * (GELU_A + (3.0 * GELU_A * GELU_B) * x2)


def ds(start, size, multiple):
    return pl.ds(pl.multiple_of(start, multiple), size)


def kernel(
    emb, w1_hbm, w2_hbm, target_hbm, vw_hbm, aw_hbm,
    ed, full,
    e, w1, w1t, w2_in, target, vw, aw, w2p, w2t, act, dg, gv, gp, tgt, vcol, av,
    fs, fr, gs, gr, grad, core_in, s1, r1, s2, s3, loss,
    in_sem, area_sem, f_sem, g_sem, core_sem, rs0_sem, rs1_sem, x_sem, ag1_sem, ag0_sem, cg_sem,
):
    me = lax.axis_index("member")
    g = lax.axis_index("grid")
    pos = {"x": me % 4, "y": (g // 8) * 2 + me // 4, "z": (g // 2) % 4, "c": g % 2}
    core = pos["c"]

    def device(p):
        return ((p["y"] % 2) * 4 + p["x"], ((p["y"] // 2) * 4 + p["z"]) * 2 + p["c"])

    def moved(**by):
        return {k: (v + by[k]) % (2 if k == "c" else 4) if k in by else v for k, v in pos.items()}

    def remote(src, dst, send_sem, recv_sem, to):
        return pltpu.make_async_remote_copy(
            src_ref=src, dst_ref=dst, send_sem=send_sem, recv_sem=recv_sem,
            device_id=to, device_id_type=MESH,
        )

    other_core = device(moved(c=1))

    def arrived(ref, sem):
        remote(ref, ref, sem, sem, other_core).wait_recv()

    def left(ref, sem):
        remote(ref, ref, sem, sem, other_core).wait_send()

    def member_peer(o):
        return (me // 4 + o // 4) % 2 * 4 + (me % 4 + o % 4) % 4

    def emb_copy(q):
        sl = pl.ds(q * CQ, CQ)
        return pltpu.make_async_copy(emb.at[:, :, sl], e.at[:, :, sl], in_sem.at[q])

    w1_copy = pltpu.make_async_copy(w1_hbm, w1, in_sem.at[NQ])
    small_copies = [
        pltpu.make_async_copy(src, dst, in_sem.at[NQ + 1 + i])
        for i, (src, dst) in enumerate(
            ((w2_hbm, w2_in), (target_hbm, target), (vw_hbm, vw), (aw_hbm, aw))
        )
    ]
    barrier = pltpu.get_barrier_semaphore()

    def load():
        for copy in small_copies:
            copy.start()
        w1_copy.start()
        emb_copy(0).start()

    def greet():
        peers = [(member_peer(o), g) for o in range(1, 8)]
        peers += [(me, (g + o) % 16) for o in range(1, 16)]
        peers += [((me + 4) % 8, (g + 8) % 16)]
        for peer in peers:
            pl.semaphore_signal(barrier, inc=1, device_id=peer, device_id_type=MESH)

    def small_operands():
        for copy in small_copies:
            copy.wait()
        wide = w2_in[...].astype(F32)
        gap = jnp.zeros((VG - VH, H), F32)
        groups = []
        for r in range(NR):
            groups += [wide[r * VH : r * VH + VH], gap]
        w2t[...] = jnp.concatenate(groups, axis=0).astype(BF16)
        w2p[...] = w2t[...].T
        t32 = target[...].astype(F32)
        columns = jnp.broadcast_to(vw[...], (128, V)).T
        for r in range(NR):
            tgt[r] = t32[r * VH : r * VH + VH]
            vcol[r] = columns[r * VH : r * VH + VH]
        av[g] = aw[...]
        loss[...] = jnp.zeros_like(loss)

    def send_area():
        for o in range(1, 16):
            remote(
                av.at[g], av.at[g], area_sem.at[0], area_sem.at[1], (me, (g + o) % 16)
            ).start()

    PEERS = (6, 2, 5, 7, 4, 1, 3)

    def send_all(q, src, dst, sem):
        for o in PEERS:
            peer = member_peer(o)
            remote(src.at[q, peer], dst.at[q, me], sem.at[NQ], sem.at[q], (peer, g)).start()
        dst[q, me] = src[q, me]

    def receive_all(q, dst, sem):
        arrived(dst.at[q, pl.ds(0, 7)], sem.at[q])

    def send_member(q, m):
        for o in PEERS:
            peer = member_peer(o)
            remote(
                fs.at[q, peer, m], fr.at[q, me, m], f_sem.at[NQ], f_sem.at[q], (peer, g)
            ).start()
        fr[q, me, m] = fs[q, me, m]

    def forward(q, members=range(MEM)):
        sl = pl.ds(q * CQ, CQ)
        if 0 in members:
            emb_copy(q).wait()
        for m in members:
            y, d = gelu_and_derivative(dot(w1t[...], e[m, :, sl]))
            act[m, :, sl] = y.astype(BF16)
            dg[m, :, sl] = d
            fc = dot(w2t[...], act[m, :, sl])
            for r in range(NR):
                for l in range(NL):
                    fs[q, r * NL + l, m] = fc[VG * r : VG * r + VH, 128 * l : 128 * l + 128]

    coef = (1.0 - (1.0 - ALPHA_FAIR) / TOTAL_MEM) / (TOTAL_MEM - 1)
    d2 = SMOOTH_WIDTH * SMOOTH_WIDTH

    def pairwise(q):
        mine_r, mine_l = me // NL, me % NL
        lanes = ds(q * CQ + mine_l * 128, 128, 128)
        area = aw[pl.ds(q * NL + mine_l, 1), :]

        def tile(rows, n):
            scale = area * vcol[mine_r, rows, :]
            t = tgt[mine_r, rows, lanes]
            f = [fr[q, k // 2, k % 2, rows, :] for k in range(TOTAL_MEM)]
            s = [None] * TOTAL_MEM
            spread = None
            for i in range(TOTAL_MEM):
                for k in range(i + 1, TOTAL_MEM):
                    d = f[i] - f[k]
                    w = d * d + d2
                    inv = lax.rsqrt(w)
                    slope = d * inv
                    s[i] = slope if s[i] is None else s[i] + slope
                    s[k] = -slope if s[k] is None else s[k] - slope
                    smooth = w * inv - SMOOTH_WIDTH
                    spread = smooth if spread is None else spread + smooth
            truth = None
            for i in range(TOTAL_MEM):
                d = f[i] - t
                w = d * d + d2
                inv = lax.rsqrt(w)
                gs[q, i // 2, i % 2, rows, :] = scale * (d * inv - coef * s[i])
                smooth = w * inv - SMOOTH_WIDTH
                truth = smooth if truth is None else truth + smooth
            loss[0:n, :] += scale * (truth / TOTAL_MEM - (coef / TOTAL_MEM) * spread)

        for i in range(0, VH, 8):
            tile(pl.ds(i, min(8, VH - i)), min(8, VH - i))

    def backward(q):
        sl = pl.ds(q * CQ, CQ)
        gap = jnp.zeros((VG - VH, 128), F32)

        for m in range(MEM):
            for l in range(NL):
                groups = []
                for r in range(NR):
                    groups += [gr[q, r * NL + l, m], gap]
                at = q * CQ + 128 * l
                gv[m, :, at : at + 128] = jnp.concatenate(groups, axis=0).astype(BF16)
            gp[m, :, sl] = (dot(w2p[...], gv[m, :, sl]) * dg[m, :, sl]).astype(BF16)

    def add_to_grad(rows, cols, new, first):
        if first:
            grad[rows, cols] = new
        else:
            grad[rows, cols] += new

    def grad_in_tile(sl, half, j, first):
        rows, cols = ds(half * HALF, HALF, HALF), ds(j * 256, 256, 256)
        new = dot_t(e[0, rows, sl], gp[0, cols, sl]) + dot_t(e[1, rows, sl], gp[1, cols, sl])
        add_to_grad(rows, cols, new, first)

    def grad_out_tile(sl, half, first):
        rows = ds(half * HALF, HALF, HALF)
        new = dot_t(act[0, rows, sl], gv[0, :, sl]) + dot_t(act[1, rows, sl], gv[1, :, sl])
        add_to_grad(rows, pl.ds(H, VP), new, first)

    def weight_gradients(q, n, half):
        sl = pl.ds(q * CQ, n * CQ)

        for j in range(4):
            grad_in_tile(sl, half, j, q == 0)

        grad_out_tile(sl, half, q == 0)

    def embedding_derivative(m, q):
        sl = pl.ds(q * 512, 512)
        ed[m, :, sl] = dot(w1[...], gp[m, :, sl]).astype(BF16)

    def cols_of(u):
        return pl.ds(u * 128, 128)

    def along(u, level, s):
        return (pos[ORDERS[u % 3][level]] + s) % 4

    def peer_of(u, level, s):
        return device(moved(**{ORDERS[u % 3][level]: s}))

    def block_rows(ks):
        begin = core * HALF
        for k, size in zip(ks, (128, 32)):
            begin = begin + k * size
        size = (128, 32)[len(ks) - 1]
        return ds(begin, size, size)

    def core_send(u):
        remote(
            grad.at[ds((1 - core) * HALF, HALF, HALF), cols_of(u)], core_in.at[:, cols_of(u)],
            core_sem.at[NU], core_sem.at[u], other_core,
        ).start()

    def core_receive(u):
        cols = cols_of(u)
        arrived(core_in.at[:, cols], core_sem.at[u])
        grad[ds(core * HALF, HALF, HALF), cols] += core_in[:, cols]
        for s in OFFSETS:
            k = along(u, 0, s)
            remote(
                grad.at[block_rows([k]), cols], s1.at[u, s - 1],
                rs0_sem.at[NU], rs0_sem.at[u], peer_of(u, 0, s),
            ).start()

    def rs0_receive(u):
        arrived(s1.at[u], rs0_sem.at[u])
        own = grad[block_rows([along(u, 0, 0)]), cols_of(u)]
        r1[u] = own + s1[u, 0] + s1[u, 1] + s1[u, 2]
        for s in OFFSETS:
            k = along(u, 1, s)
            remote(
                r1.at[u, ds(k * 32, 32, 32)], s2.at[u, s - 1],
                rs1_sem.at[NU], rs1_sem.at[u], peer_of(u, 1, s),
            ).start()

    def rs1_receive(u):
        arrived(s2.at[u], rs1_sem.at[u])
        own = r1[u, ds(along(u, 1, 0) * 32, 32, 32)]
        k = along(u, 2, 0)
        s3[u, k] = own + s2[u, 0] + s2[u, 1] + s2[u, 2]
        for s in OFFSETS:
            remote(
                s3.at[u, k], s3.at[u, k], x_sem.at[NU], x_sem.at[u], peer_of(u, 2, s)
            ).start()

    rescale = 1.0 / math.sqrt(TOTAL_MEM * TOTAL_CELLS)

    def x_receive(u):
        arrived(s3.at[u, pl.ds(0, 3)], x_sem.at[u])
        at = (block_rows([along(u, 0, 0), along(u, 1, 0)]), cols_of(u))
        full[at] = (s3[u, 0] + s3[u, 1] + s3[u, 2] + s3[u, 3]) * rescale
        for s in OFFSETS:
            remote(
                full.at[at], full.at[at], ag1_sem.at[NU], ag1_sem.at[u], peer_of(u, 1, s)
            ).start()

    def to_core(u, s):
        at = (block_rows([along(u, 0, s)]), cols_of(u))
        remote(full.at[at], full.at[at], cg_sem.at[1], cg_sem.at[0], other_core).start()

    def ag1_receive(u):
        arrived(full.at[pl.ds(0, 96), cols_of(u)], ag1_sem.at[u])
        at = (block_rows([along(u, 0, 0)]), cols_of(u))
        for s in OFFSETS:
            sem = ag0_sem.at[u if u < NU - 3 else single(u, s)]
            remote(full.at[at], full.at[at], ag0_sem.at[NU], sem, peer_of(u, 0, s)).start()
        to_core(u, 0)

    def ag0_receive(u):
        arrived(full.at[pl.ds(0, 384), cols_of(u)], ag0_sem.at[u])
        for s in OFFSETS:
            to_core(u, s)

    def single(u, s):
        return NU + 1 + (u - (NU - 3)) * 3 + s - 1

    def ag0_receive_block(u, s):
        at = full.at[block_rows([along(u, 0, 4 - s)]), cols_of(u)]
        arrived(at, ag0_sem.at[single(u, s)])
        to_core(u, 4 - s)

    def run():
        load()
        greet()
        small_operands()
        w1_copy.wait()
        for q in range(1, NQ):
            emb_copy(q).start()
        w1t[...] = w1[...].T
        forward(0, (0,))
        pl.semaphore_wait(barrier, 23)
        send_member(0, 0)
        forward(0, (1,))
        send_member(0, 1)
        send_area()
        forward(1)
        send_all(1, fs, fr, f_sem)
        forward(2)
        send_all(2, fs, fr, f_sem)
        arrived(av.at[pl.ds(0, 15)], area_sem.at[1])
        mean = jnp.sum(jnp.sum(av[...], axis=0), keepdims=True) / TOTAL_CELLS
        aw[...] = aw[...] / mean
        receive_all(0, fr, f_sem)
        pairwise(0)
        send_all(0, gs, gr, g_sem)
        forward(3)
        send_all(3, fs, fr, f_sem)
        receive_all(1, fr, f_sem)
        pairwise(1)
        send_all(1, gs, gr, g_sem)
        receive_all(2, fr, f_sem)
        pairwise(2)
        send_all(2, gs, gr, g_sem)
        receive_all(0, gr, g_sem)
        backward(0)
        receive_all(3, fr, f_sem)
        pairwise(3)
        send_all(3, gs, gr, g_sem)
        receive_all(1, gr, g_sem)
        backward(1)
        weight_gradients(0, 2, 0)
        weight_gradients(0, 2, 1)
        receive_all(2, gr, g_sem)
        backward(2)
        receive_all(3, gr, g_sem)
        backward(3)
        own_loss = jnp.sum(loss[...], keepdims=True)
        row = lax.broadcasted_iota(jnp.int32, (8, VP), 0)
        col = lax.broadcasted_iota(jnp.int32, (8, VP), 1)
        grad[0:8, H:WIDE] += jnp.where((row == 0) & (col == LOSS_COL), own_loss, 0.0)
        last = pl.ds(2 * CQ, 2 * CQ)
        for j in range(4):
            grad_in_tile(last, 1 - core, j, False)
            core_send(2 * j)
            core_send(2 * j + 1)
        grad_out_tile(last, 1 - core, False)
        core_send(NU - 1)
        grad_in_tile(last, core, 0, False)
        core_receive(0)
        grad_in_tile(last, core, 1, False)
        core_receive(1)
        grad_in_tile(last, core, 2, False)
        core_receive(2)
        core_receive(3)
        grad_in_tile(last, core, 3, False)
        core_receive(4)
        grad_out_tile(last, core, False)
        core_receive(5)
        waves = ((0, 1, 2), (3, 4, 5), (6, 7, 8))

        def each(step, wave):
            for u in waves[wave]:
                step(u)

        embedding_derivative(0, 0)
        each(rs0_receive, 0)
        each(core_receive, 2)
        embedding_derivative(1, 0)
        each(rs0_receive, 1)
        each(rs1_receive, 0)
        embedding_derivative(0, 1)
        each(rs0_receive, 2)
        each(rs1_receive, 1)
        each(x_receive, 0)
        each(rs1_receive, 2)
        each(x_receive, 1)
        each(ag1_receive, 0)
        each(x_receive, 2)
        embedding_derivative(1, 1)
        each(ag1_receive, 1)
        each(ag1_receive, 2)
        each(ag0_receive, 0)
        each(ag0_receive, 1)
        for s in (1, 3, 2):
            for u in waves[2]:
                ag0_receive_block(u, s)
        arrived(full.at[pl.ds(0, HALF)], cg_sem.at[0])

    run()
    left(av.at[pl.ds(0, 15)], area_sem.at[0])
    left(fs.at[:, pl.ds(0, 7)], f_sem.at[NQ])
    left(gs.at[:, pl.ds(0, 7)], g_sem.at[NQ])
    left(core_in, core_sem.at[NU])
    left(s1, rs0_sem.at[NU])
    left(s2, rs1_sem.at[NU])
    left(s3.at[:, pl.ds(0, 3)], x_sem.at[NU])
    left(s2, ag1_sem.at[NU])
    left(s1, ag0_sem.at[NU])
    left(core_in, cg_sem.at[1])


def finish(ed, full, ed_out, grad_out, grad_t_out, penalty, sem):
    ed_copy = pltpu.make_async_copy(ed, ed_out, sem.at[0])
    ed_copy.start()
    grad_copy = pltpu.make_async_copy(full.at[:, 0:H], grad_out, sem.at[1])
    grad_copy.start()
    t = full[:, H:WIDE].T
    grad_t_out[...] = jnp.concatenate([t[VG * r : VG * r + VH] for r in range(NR)], axis=0)
    rescale = 1.0 / math.sqrt(TOTAL_MEM * TOTAL_CELLS)
    at = full[0:1, H + LOSS_COL : H + LOSS_COL + 1]
    penalty[...] = at * (1.0 / (rescale * TOTAL_CELLS * V))
    ed_copy.wait()
    grad_copy.wait()


def per_device(
    embedding_tensor,
    first_projection_matrix,
    variable_projection_matrix,
    target,
    var_weight,
    area_weight,
):
    vmem = pl.BlockSpec(memory_space=pltpu.VMEM)
    hbm = pl.BlockSpec(memory_space=pl.ANY)
    dma = pltpu.SemaphoreType.DMA
    big = (MEM, H, CELLS)
    swap = (NQ, 8, MEM, VH, 128)
    in_vmem = (pltpu.VMEM(big, BF16), pltpu.VMEM((H, WIDE), F32))
    ed, full = pl.pallas_call(
        kernel,
        name="decoder_crps",
        out_shape=in_vmem,
        in_specs=[hbm] * 6,
        out_specs=(vmem, vmem),
        scratch_shapes=[
            pltpu.VMEM(big, BF16),
            pltpu.VMEM((H, H), BF16),
            pltpu.VMEM((H, H), BF16),
            pltpu.VMEM((V, H), BF16),
            pltpu.VMEM((V, CELLS), BF16),
            pltpu.VMEM((1, V), F32),
            pltpu.VMEM((8, 128), F32),
            pltpu.VMEM((H, VP), BF16),
            pltpu.VMEM((VP, H), BF16),
            pltpu.VMEM(big, BF16),
            pltpu.VMEM(big, F32),
            pltpu.VMEM((MEM, VP, CELLS), BF16),
            pltpu.VMEM(big, BF16),
            pltpu.VMEM((NR, VH, CELLS), F32),
            pltpu.VMEM((NR, VH, 128), F32),
            pltpu.VMEM((16, 8, 128), F32),
            pltpu.VMEM(swap, F32),
            pltpu.VMEM(swap, F32),
            pltpu.VMEM(swap, F32),
            pltpu.VMEM(swap, F32),
            pltpu.VMEM((H, WIDE), F32),
            pltpu.VMEM((HALF, WIDE), F32),
            pltpu.VMEM((NU, 3, 128, 128), F32),
            pltpu.VMEM((NU, 128, 128), F32),
            pltpu.VMEM((NU, 3, 32, 128), F32),
            pltpu.VMEM((NU, 4, 32, 128), F32),
            pltpu.VMEM((8, 128), F32),
            dma((NQ + 5,)),
            dma((2,)),
            dma((NQ + 1,)), dma((NQ + 1,)),
            dma((NU + 1,)), dma((NU + 1,)), dma((NU + 1,)), dma((NU + 1,)),
            dma((NU + 1,)), dma((NU + 10,)), dma((2,)),
        ],
        compiler_params=pltpu.CompilerParams(
            collective_id=0, has_side_effects=True, vmem_limit_bytes=50 * 2**20
        ),
        cost_estimate=pl.CostEstimate(
            flops=15_000_000_000, bytes_accessed=20_000_000, transcendentals=4_000_000
        ),
    )(
        embedding_tensor,
        first_projection_matrix,
        variable_projection_matrix.T,
        target,
        var_weight.reshape(1, V),
        area_weight.reshape(8, 128),
    )
    ed, grad_in, grad_out_t, penalty = pl.pallas_call(
        finish,
        name="write_out",
        out_shape=(
            jax.ShapeDtypeStruct(big, BF16),
            jax.ShapeDtypeStruct((H, H), F32),
            jax.ShapeDtypeStruct((V, H), F32),
            jax.ShapeDtypeStruct((1, 1), F32),
        ),
        in_specs=[vmem, vmem],
        out_specs=(hbm, hbm, vmem, vmem),
        scratch_shapes=[dma((2,))],
        compiler_params=pltpu.CompilerParams(vmem_limit_bytes=8 * 2**20),
    )(ed, full)
    return ed, grad_in, grad_out_t.T, penalty[0, 0]


def solution(mesh):
    in_specs = (P("member", None, "grid"), P(), P(), P(None, "grid"), P(), P("grid"))
    out_specs = (P("member", None, "grid"), P(), P(), P())
    return jax.shard_map(
        per_device, mesh=mesh, in_specs=in_specs, out_specs=out_specs, check_vma=False
    )
```
